128 devices in a mesh: ctx: 32 (over y, x, core), head: 4 (over z).
Axes of the slice: x: 4, y: 4, z: 4, core: 2. Of those that a mesh axis runs over, the one named last changes fastest.
Arguments:
- queries: bfloat16 [65536, 2048], P('ctx', 'head'), may hold values from -6 to 6
- key_rows: bfloat16 [65536, 2048], P('ctx', 'head'), may hold values from -6 to 6
- value_rows: bfloat16 [65536, 2048], P('ctx', 'head'), may hold values from -6 to 6
- level_codes: int32 [65536, 21], P('ctx'), may hold values from 0 to 15
- level_coefs: float32 [16, 16], P('head'), may hold values from 0.1 to 1
- norm_gain: float32 [2048], P('head'), may hold values from 0.1 to 1.9
- w_query: bfloat16 [2048, 2048], replicated, may hold values from -1 to 1
- w_key: bfloat16 [2048, 512], replicated, may hold values from -1 to 1
- w_value: bfloat16 [2048, 512], replicated, may hold values from -0.125 to 0.125
- lookback: int32 [65536], P(('ctx', 'head')), may hold values from 0 to 256
Outputs:
- fenwick_out: bfloat16 [65536, 2048], P('ctx', 'head')
- attended: bfloat16 [65536, 2048], P(('ctx', 'head'))
The draws below stay inside these ranges and needn't reach their ends.
All inputs are finite; a program needn't handle non-finite values.
Results may differ from the reference program's by a relative error of at most 0.014.
Values may be sent and summed in bfloat16 or wider, within the bound.
A program may use at most 192 MiB of HBM per device.

```python
import math
import jax
import jax.numpy as jnp
from jax import lax

HD = 128
HEADS = 16
KV_HEADS = 4
D = 2048
KVD = 512
TOK_DEV = 2048
TOKENS = 65536
WIN = 256
LEVELS = 21
NCOEF = 16
N_CTX = 32
N_HEAD = 4


def draw_w_query(key, part):
    key = jax.random.fold_in(key, 11)
    others = jax.random.normal(key, (D, KV_HEADS, HEADS // KV_HEADS, HD), jnp.float32)
    scaled = jnp.clip(others * D ** (-0.5), -1.0, 1.0)
    return scaled.reshape(D, HEADS * HD).astype(jnp.bfloat16)


def draw_w_key(key, part):
    key = jax.random.fold_in(key, 12)
    noise = jax.random.normal(key, (D, KV_HEADS, HD), jnp.float32)
    mixed_cols = noise
    scaled = jnp.clip(mixed_cols * D ** (-0.5), -1.0, 1.0)
    return scaled.reshape(D, KV_HEADS * HD).astype(jnp.bfloat16)


def plant(array, own_key, least, largest):
    longest = array.shape.index(max(array.shape))
    spots = []
    for shift in (0, 1):
        where = [jax.random.randint(jax.random.fold_in(own_key, axis), (), 0, length) for axis, length in enumerate(array.shape)]
        where[longest] = (where[longest] + shift) % array.shape[longest]
        spots.append(tuple(where))
    return array.at[spots[0]].set(least).at[spots[1]].set(largest)


def levels(stream_key, extent, shards, low, largest):
    def one(axis_at, parts):
        heights = jax.random.uniform(jax.random.fold_in(jax.random.fold_in(stream_key, 6), axis_at), (parts,), jnp.float32, low / len(shards), largest / len(shards))
        return jnp.repeat(jnp.exp(heights), extent[axis_at] // parts).reshape((-1,) + (1,) * (len(extent) - axis_at - 1))

    factor_of = one(*shards[0])
    for cut in shards[1:]:
        factor_of = factor_of * one(*cut)
    return factor_of


def gaussian(own_key, dims, spread, most, pieces=(), kind=jnp.bfloat16):
    array = spread * jax.random.normal(own_key, dims, jnp.float32)
    if pieces:
        array = array * levels(own_key, dims, pieces, -0.22, 0.18)
    return jnp.clip(array, -most, most).astype(kind)


def setup_inputs(seed: int = 0) -> dict:
    key_list = jax.random.split(jax.random.key(seed), 11)
    queries = gaussian(key_list[0], (TOKENS, D), 1.0, 6.0, ((0, 32), (1, 4)))
    key_rows = gaussian(key_list[1], (TOKENS, D), 1.0, 6.0, ((0, 32), (1, 4)))
    value_rows = gaussian(key_list[2], (TOKENS, D), 1.0, 6.0, ((0, 32), (1, 4)))
    level_codes = plant(jax.random.randint(key_list[3], (TOKENS, LEVELS), 0, NCOEF), jax.random.fold_in(key_list[3], 1), 0, NCOEF - 1).astype(jnp.int32)
    level_coefs = jnp.clip(jnp.exp(math.log(1.0) - 2.3025851 * jax.random.uniform(key_list[4], (HEADS, NCOEF), jnp.float32) ** levels(key_list[4], (HEADS, NCOEF), ((0, 4),), -0.2, 0.2)), 0.1, 1.0)
    norm_gain = jnp.clip(1.0 + 0.18 * jax.random.normal(key_list[5], (D,), jnp.float32), 0.1, 1.9)
    w_query = draw_w_query(jax.random.fold_in(key_list[10], 71), 0)
    w_key = draw_w_key(jax.random.fold_in(key_list[10], 71), 0)
    w_value = gaussian(key_list[8], (D, KVD), D ** -0.5, 0.125)
    lookback = plant(jax.random.randint(key_list[9], (TOKENS,), 0, WIN + 1), jax.random.fold_in(key_list[9], 1), 0, WIN).astype(jnp.int32)
    return dict(queries=queries, key_rows=key_rows, value_rows=value_rows, level_codes=level_codes, level_coefs=level_coefs, norm_gain=norm_gain, w_query=w_query, w_key=w_key, w_value=w_value, lookback=lookback)


precise = lax.Precision.HIGHEST

def span_level(bit_diff, bits):
    level_total = jnp.zeros(bit_diff.shape, jnp.int32)
    for shift_by in range(bits):
        level_total = level_total + (jnp.right_shift(bit_diff, shift_by) > 0).astype(jnp.int32)
    return level_total

def fenwick_block(query3, key3, value3, level_w, remote, head_gain, tok_bits, ctx_bits):
    tok_count = query3.shape[0]
    heads_here = query3.shape[1]
    block_rows = min(512, tok_count)
    score_scale = HD ** (-0.5)
    positions = jnp.arange(tok_count, dtype=jnp.int32)
    near_parts = []
    for row_first in range(0, tok_count, block_rows):
        row_last = row_first + block_rows
        scores = jnp.einsum('qhd,khd->hqk', query3[row_first:row_last].astype(jnp.float32), key3.astype(jnp.float32)) * score_scale
        level_ids = span_level(jnp.bitwise_xor(positions[row_first:row_last, None], positions[None, :]), tok_bits)
        picked = jnp.take_along_axis(level_w[:, row_first:row_last, :], jnp.broadcast_to(level_ids[None], (heads_here, block_rows, tok_count)), axis=2)
        causal = positions[None, :] <= positions[row_first:row_last, None]
        terms = jnp.where(causal[None], scores * picked, 0.0).astype(jnp.bfloat16)
        near_parts.append(jnp.einsum('hqk,khe->qhe', terms.astype(jnp.float32), value3.astype(jnp.float32)))
    near_terms = jnp.concatenate(near_parts, axis=0)
    remote_bf = remote.astype(jnp.bfloat16)
    far_lam = jnp.transpose(level_w[:, :, tok_bits + 1:tok_bits + 1 + ctx_bits], (1, 0, 2))
    scaled_q = (query3.astype(jnp.float32)[:, :, None, :] * far_lam[:, :, :, None]).astype(jnp.bfloat16)
    far_sum = jnp.einsum('thjd,jhde->the', scaled_q.astype(jnp.float32), remote_bf.astype(jnp.float32), precision=precise)
    loglin = near_terms + score_scale * far_sum
    mean_sq = lax.optimization_barrier(jnp.mean(loglin * loglin, axis=-1, keepdims=True))
    normed = loglin * lax.rsqrt(mean_sq + 1e-06) * head_gain
    return normed.astype(jnp.bfloat16)

def reference(queries, key_rows, value_rows, level_codes, level_coefs, norm_gain, w_query, w_key, w_value, lookback):
    tok_bits = TOK_DEV.bit_length() - 1
    ctx_bits = N_CTX.bit_length() - 1
    level_weights = level_coefs[:, level_codes]
    query4 = queries.reshape(N_CTX, TOK_DEV, HEADS, HD)
    key4 = key_rows.reshape(N_CTX, TOK_DEV, HEADS, HD)
    value4 = value_rows.reshape(N_CTX, TOK_DEV, HEADS, HD)

    def state_of(kv_pair):
        return jnp.einsum('thd,the->hde', kv_pair[0].astype(jnp.float32), kv_pair[1].astype(jnp.float32))
    states = lax.map(state_of, (key4, value4))
    shard_ids = jnp.arange(N_CTX, dtype=jnp.int32)
    reach_levels = span_level(jnp.bitwise_xor(shard_ids[:, None], shard_ids[None, :]), ctx_bits)
    wanted = jnp.arange(1, ctx_bits + 1, dtype=jnp.int32)
    picker = ((shard_ids[None, None, :] < shard_ids[:, None, None]) & (reach_levels[:, None, :] == wanted[None, :, None])).astype(jnp.float32)
    remote = jnp.einsum('cjx,xhde->cjhde', picker, states, precision=precise)
    weights4 = jnp.transpose(level_weights.reshape(HEADS, N_CTX, TOK_DEV, LEVELS), (1, 0, 2, 3))
    head_gain = norm_gain.reshape(HEADS, HD)

    def one_block(block_items):
        return fenwick_block(block_items[0], block_items[1], block_items[2], block_items[3], block_items[4], head_gain, tok_bits, ctx_bits)
    fenwick_out = lax.map(one_block, (query4, key4, value4, weights4, remote)).reshape(TOKENS, D)
    seg_rows = TOK_DEV // N_HEAD
    groups = HEADS // KV_HEADS
    score_scale = HD ** (-0.5)
    query_all = jnp.dot(fenwick_out, w_query, preferred_element_type=jnp.float32).astype(jnp.bfloat16)
    key_all = jnp.dot(fenwick_out, w_key, preferred_element_type=jnp.float32).astype(jnp.bfloat16)
    value_all = jnp.dot(fenwick_out, w_value, preferred_element_type=jnp.float32).astype(jnp.bfloat16)
    padding = jnp.zeros((WIN, KVD), jnp.bfloat16)
    key_pad = jnp.concatenate([padding, key_all], axis=0)
    value_pad = jnp.concatenate([padding, value_all], axis=0)

    def window_block(row_first):
        rows_q = lax.dynamic_slice_in_dim(query_all, row_first, seg_rows).reshape(seg_rows, KV_HEADS, groups, HD)
        keys_here = lax.dynamic_slice_in_dim(key_pad, row_first, seg_rows + WIN).reshape(seg_rows + WIN, KV_HEADS, HD)
        values_here = lax.dynamic_slice_in_dim(value_pad, row_first, seg_rows + WIN).reshape(seg_rows + WIN, KV_HEADS, HD)
        window_back = lax.dynamic_slice_in_dim(lookback, row_first, seg_rows)
        t_pos = row_first + jnp.arange(seg_rows, dtype=jnp.int32)
        k_pos = row_first - WIN + jnp.arange(seg_rows + WIN, dtype=jnp.int32)
        scores = jnp.einsum('sgcd,kgd->gcsk', rows_q.astype(jnp.float32), keys_here.astype(jnp.float32)) * score_scale
        valid = (k_pos[None, :] <= t_pos[:, None]) & (k_pos[None, :] >= t_pos[:, None] - window_back[:, None]) & (k_pos[None, :] >= 0)
        scores = jnp.where(valid[None, None], scores, -1e+30)
        row_max = lax.optimization_barrier(jnp.max(scores, axis=-1, keepdims=True))
        exps = jnp.exp(scores - row_max)
        weights_bf = (exps / lax.optimization_barrier(jnp.sum(exps, axis=-1, keepdims=True))).astype(jnp.bfloat16)
        rows_out = jnp.einsum('gcsk,kgd->sgcd', weights_bf.astype(jnp.float32), values_here.astype(jnp.float32))
        return rows_out.astype(jnp.bfloat16).reshape(seg_rows, D)
    starts = jnp.arange(TOKENS // seg_rows, dtype=jnp.int32) * seg_rows
    attended = lax.map(window_block, starts).reshape(TOKENS, D)
    return (fenwick_out, attended)
```

```python
import functools

import jax
import jax.numpy as jnp
from jax import lax
from jax.experimental import pallas as pl
from jax.experimental.pallas import tpu as pltpu
from jax.sharding import PartitionSpec as P

HD = 128
HEADS = 16
KV_HEADS = 4
GROUPS = HEADS // KV_HEADS
WIN = 256
NCOEF = 16
N_HEAD = 4
SIDE = 4
FAR = 5
HERE = HEADS // N_HEAD
CHUNK = 256
HALF = CHUNK // 2
ROWS = 128
NEAR_BITS = 8
MESH = pl.DeviceIdType.MESH
BF = jnp.bfloat16
F32 = jnp.float32
SCALE = HD ** (-0.5)
LOG2E = 1.4426950408889634


def mm(a, b):
    return jnp.dot(a, b, preferred_element_type=F32)


def mm_nt(a, b):
    return lax.dot_general(a, b, (((1,), (1,)), ((), ())), preferred_element_type=F32)


def body(
    q_hbm, k_hbm, v_hbm, codes_hbm, coef_hbm, gain_hbm, wq_hbm, wk_hbm, wv_hbm, look_hbm,
    fen_hbm, att_hbm,
    q_v, k_v, v_v, qt, vt, codes, coef, gain, gain_t, look, lam, lev, loc, cst, lst,
    tot, totb, crecv, xr, yr, far, fen, xg, w_v, qs, kvb, bias, att,
    in_sem, w_sem, out_sem, small_sem,
    core_ss, core_rs, x_ss, x_rs, y_ss, y_rs, f_ss, f_rs, z_ss, z_rs, h_ss, h_rs,
):
    tok = q_hbm.shape[0]
    chunks = tok // CHUNK
    seg = tok // N_HEAD
    d_model = wq_hbm.shape[0]
    kvd = wk_hbm.shape[1]
    feat = HERE * HD
    n_ctx = lax.axis_size("ctx")

    c = lax.axis_index("ctx")
    z = lax.axis_index("head")
    core = lax.rem(c, 2)
    cx = lax.rem(c // 2, SIDE)
    cy = c // (2 * SIDE)
    shard = c * N_HEAD + z

    def at_x(v):
        return (cy * 2 * SIDE + v * 2 + core, z)

    def at_y(v):
        return (v * 2 * SIDE + cx * 2 + core, z)

    def at_z(v):
        return (c, v)

    other_core = (c + 1 - 2 * core, z)
    nshard = n_ctx * N_HEAD
    nxt = lax.rem(shard + 1, nshard)
    prv = lax.rem(shard + nshard - 1, nshard)
    next_dev = (nxt // N_HEAD, lax.rem(nxt, N_HEAD))
    prev_dev = (prv // N_HEAD, lax.rem(prv, N_HEAD))

    half_tok = tok // 2
    first = []
    for n in range(2):
        rows = pl.ds(n * half_tok, half_tok)
        pair = []
        for a, (src, dst) in enumerate(((v_hbm, v_v), (k_hbm, k_v))):
            cp = pltpu.make_async_copy(src.at[rows], dst.at[rows], in_sem.at[n, a])
            cp.start()
            pair.append(cp)
        first.append(pair)
    small = []
    for a, (src, dst) in enumerate(
        ((codes_hbm, codes), (coef_hbm, coef), (gain_hbm, gain), (look_hbm, look))
    ):
        cp = pltpu.make_async_copy(src, dst, small_sem.at[a])
        cp.start()
        small.append(cp)
    q_in = pltpu.make_async_copy(q_hbm, q_v, in_sem.at[2, 0])
    q_in.start()
    w_in = [
        pltpu.make_async_copy(wk_hbm, w_v.at[:, pl.ds(d_model, kvd)], w_sem.at[0]),
        pltpu.make_async_copy(wv_hbm, w_v.at[:, pl.ds(d_model + kvd, kvd)], w_sem.at[1]),
        pltpu.make_async_copy(wq_hbm, w_v.at[:, pl.ds(0, d_model)], w_sem.at[2]),
    ]
    for cp in w_in:
        cp.start()

    barrier = pltpu.get_barrier_semaphore()
    friends = [other_core, next_dev, prev_dev]
    for s in range(1, SIDE):
        friends.append(at_x(lax.rem(cx + s, SIDE)))
        friends.append(at_y(lax.rem(cy + s, SIDE)))
        friends.append(at_z(lax.rem(z + s, N_HEAD)))
    for dev in friends:
        pl.semaphore_signal(barrier, inc=1, device_id=dev, device_id_type=MESH)

    for n in range(2):
        for cp in first[n]:
            cp.wait()

        def state_step(i, carry, n=n):
            start = pl.multiple_of(i * CHUNK, CHUNK)
            rows = pl.ds(start, CHUNK)
            vtc = v_v[rows, :].T
            vt[:, rows] = vtc
            for h in range(HERE):
                hs = slice(h * HD, (h + 1) * HD)
                cst[i, hs, :] = mm(vtc[hs, :], k_v[rows, hs])
            return carry

        lax.fori_loop(n * chunks // 2, (n + 1) * chunks // 2, state_step, 0)

    pairs = [cst[2 * j] + cst[2 * j + 1] for j in range(4)]
    lo4 = pairs[0] + pairs[1]
    total = lo4 + (pairs[2] + pairs[3])
    tot[...] = total
    totb[...] = total.astype(BF)
    for j in range(4):
        lst[j] = cst[2 * j].astype(BF)
    lst[4] = pairs[0].astype(BF)
    lst[5] = pairs[2].astype(BF)
    lst[6] = lo4.astype(BF)

    pl.semaphore_wait(barrier, len(friends))
    core_cp = pltpu.make_async_remote_copy(
        src_ref=totb, dst_ref=crecv, send_sem=core_ss.at[0], recv_sem=core_rs.at[0],
        device_id=other_core, device_id_type=MESH,
    )
    core_cp.start()

    for cp in small:
        cp.wait()
    si = lax.broadcasted_iota(jnp.int32, (HALF, HALF), 0)
    ti = lax.broadcasted_iota(jnp.int32, (HALF, HALF), 1)
    diff = jnp.bitwise_xor(si, ti)
    level = jnp.zeros((HALF, HALF), jnp.int32)
    for b in range(NEAR_BITS - 1):
        level = level + jnp.where(diff >= (1 << b), 1, 0)
    lev[...] = jnp.where(si <= ti, level, 99)
    for h in range(HERE):
        gain_t[h * HD : (h + 1) * HD, :] = jnp.broadcast_to(gain[h : h + 1, :], (HD, HD)).T

    my_half = pl.multiple_of(core * (feat // 2), feat // 2)
    half_rows = pl.ds(my_half, feat // 2)

    core_cp.wait_recv()
    xr[cx] = (tot[half_rows, :] + crecv[half_rows, :].astype(F32)).astype(BF)
    x_cps = []
    for s in (2, 1, 3):
        cp = pltpu.make_async_remote_copy(
            src_ref=xr.at[cx], dst_ref=xr.at[cx], send_sem=x_ss.at[s], recv_sem=x_rs.at[s],
            device_id=at_x(lax.rem(cx + s, SIDE)), device_id_type=MESH,
        )
        cp.start()
        x_cps.append(cp)
    far[:, 0:HD] = jnp.where(core == 1, crecv[...].astype(F32), 0.0).astype(BF)

    def lam_step(i, carry):
        cols = pl.ds(pl.multiple_of(i * CHUNK, CHUNK), CHUNK)
        cd = codes[:, cols]
        for h in range(HERE):
            acc = jnp.full(cd.shape, coef[h, 0], F32)
            for n in range(1, NCOEF):
                acc = jnp.where(cd == n, coef[h, n], acc)
            lam[h, :, cols] = acc
        return carry

    lax.fori_loop(0, chunks, lam_step, 0)
    q_in.wait()

    def q_step(i, carry):
        rows = pl.ds(pl.multiple_of(i * CHUNK, CHUNK), CHUNK)
        qt[:, rows] = q_v[rows, :].T
        return carry

    lax.fori_loop(0, chunks, q_step, 0)

    def local_chunk(i):
        t0 = i * CHUNK
        cols = slice(t0, t0 + CHUNK)

        def head(h, carry):
            hoff = pl.multiple_of(h * HD, HD)
            hrows = pl.ds(hoff, HD)
            qth = qt[hrows, cols]
            st = mm(k_v[cols, hrows], qth)
            lamh = lam.at[h]

            def quad(a):
                lo = t0 + a * HALF
                w = jnp.zeros((HALF, HALF), F32)
                lv = lev[...]
                for l in range(NEAR_BITS):
                    w = jnp.where(lv == l, lamh[l : l + 1, lo : lo + HALF], w)
                return (st[a * HALF : (a + 1) * HALF, a * HALF : (a + 1) * HALF] * w).astype(BF)

            cross = (
                st[:HALF, HALF:] * lamh[NEAR_BITS : NEAR_BITS + 1, t0 + HALF : t0 + CHUNK]
            ).astype(BF)
            top = jnp.concatenate([quad(0), cross], axis=1)
            low = jnp.concatenate([jnp.zeros((HALF, HALF), BF), quad(1)], axis=1)
            terms = jnp.concatenate([top, low], axis=0)
            acc = mm(vt[hrows, cols], terms)
            used = []
            if i & 1:
                used.append((i // 2, 9))
            if i & 2:
                used.append((4 + i // 4, 10))
            if i & 4:
                used.append((6, 11))
            for slot, l in used:
                ql = qth * jnp.broadcast_to(lamh[l : l + 1, cols], (HD, CHUNK)).astype(BF)
                acc = acc + mm(lst[slot, hrows, :], ql)
            loc[hrows, cols] = acc
            return carry

        lax.fori_loop(0, HERE, head, 0)

    for i in (7, 6):
        local_chunk(i)

    for cp in x_cps:
        cp.wait_recv()

    def m(cond):
        return jnp.where(cond, 1.0, 0.0).astype(F32)

    def level_pair(buf, pos):
        parts = [buf[j].astype(F32) for j in range(SIDE)]
        low = parts[0] + parts[1]
        one = parts[0] * m(pos == 1) + parts[2] * m(pos == 3)
        two = low * m(pos >= 2)
        return one.astype(BF), two.astype(BF), low + (parts[2] + parts[3])

    one, two, row_sum = level_pair(xr, cx)
    yr[cy] = row_sum.astype(BF)
    y_cps = []
    for s in (2, 1, 3):
        cp = pltpu.make_async_remote_copy(
            src_ref=yr.at[cy], dst_ref=yr.at[cy], send_sem=y_ss.at[s], recv_sem=y_rs.at[s],
            device_id=at_y(lax.rem(cy + s, SIDE)), device_id_type=MESH,
        )
        cp.start()
        y_cps.append(cp)
    far[half_rows, HD : 2 * HD] = one
    far[half_rows, 2 * HD : 3 * HD] = two

    def pass_on(n):
        piece = far.at[half_rows, pl.ds((2 * n + 1) * HD, 2 * HD)]
        cp = pltpu.make_async_remote_copy(
            src_ref=piece, dst_ref=piece, send_sem=f_ss.at[n], recv_sem=f_rs.at[n],
            device_id=other_core, device_id_type=MESH,
        )
        cp.start()
        return cp

    f_cps = [pass_on(0)]

    for i in (5, 4, 3, 2, 1, 0):
        local_chunk(i)

    ri = lax.broadcasted_iota(jnp.int32, (ROWS, WIN + ROWS), 0)
    ji = lax.broadcasted_iota(jnp.int32, (ROWS, WIN + ROWS), 1)
    gap = WIN + ri - ji
    for b in range(seg // ROWS):
        reach = jnp.broadcast_to(look[b : b + 1, :].astype(F32), (ROWS, ROWS)).T
        reach = jnp.concatenate([reach] * 3, axis=1).astype(jnp.int32)
        key_pos = shard * seg + b * ROWS - WIN + ji
        ok = (gap >= 0) & (gap <= reach) & (key_pos >= 0)
        bias[b] = jnp.where(ok, 0.0, -1e30)

    for cp in y_cps:
        cp.wait_recv()
    one, two, _ = level_pair(yr, cy)
    far[half_rows, 3 * HD : 4 * HD] = one
    far[half_rows, 4 * HD : 5 * HD] = two
    f_cps.append(pass_on(1))
    for cp in f_cps:
        cp.wait()

    def chunk_of(n):
        hf = 1 - n // N_HEAD
        j = lax.rem(n, N_HEAD)
        k = jnp.where(j == 0, 2, jnp.where(j == 1, 1, jnp.where(j == 2, 3, 0)))
        dest = lax.rem(z + k, N_HEAD)
        return hf, k, dest

    def z_copy(hf, k, dest):
        src_rows = pl.ds(pl.multiple_of(dest * seg + hf * CHUNK, CHUNK), CHUNK)
        return pltpu.make_async_remote_copy(
            src_ref=fen.at[src_rows],
            dst_ref=xg.at[
                pl.ds(pl.multiple_of(hf * CHUNK, CHUNK), CHUNK),
                pl.ds(pl.multiple_of(z * feat, feat), feat),
            ],
            send_sem=z_ss.at[hf, k],
            recv_sem=z_rs.at[hf, k],
            device_id=at_z(dest),
            device_id_type=MESH,
        )

    def far_step(n, carry):
        hf, k, dest = chunk_of(n)
        start = pl.multiple_of(dest * seg + hf * CHUNK, CHUNK)
        cols = pl.ds(start, CHUNK)
        for h in range(HERE):
            hs = slice(h * HD, (h + 1) * HD)
            qth = qt[hs, cols]
            parts = []
            for l in range(FAR):
                row = lam[h, 12 + l : 13 + l, cols]
                parts.append(qth * jnp.broadcast_to(row, (HD, CHUNK)).astype(BF))
            acc = loc[hs, cols] + mm(far[hs, :], jnp.concatenate(parts, axis=0))
            ms = jnp.sum(acc * acc, axis=0, keepdims=True)
            r = SCALE * lax.rsqrt(ms * (SCALE * SCALE / HD) + 1e-06)
            g = gain_t[hs, :]
            g = jnp.concatenate([g, g], axis=1)
            fen[cols, hs] = (acc * r * g).astype(BF).T

        @pl.when(k > 0)
        def _():
            z_copy(hf, k, dest).start()

        @pl.when(k == 0)
        def _():
            xg[
                pl.ds(pl.multiple_of(hf * CHUNK, CHUNK), CHUNK),
                pl.ds(pl.multiple_of(z * feat, feat), feat),
            ] = fen[cols, :]

        return carry

    lax.fori_loop(0, 2 * N_HEAD, far_step, 0)
    fen_out = pltpu.make_async_copy(fen, fen_hbm, out_sem.at[0])
    fen_out.start()
    for cp in w_in:
        cp.wait()

    def arrive(hf):
        for k in range(1, N_HEAD):
            z_copy(hf, k, lax.rem(z + k, N_HEAD)).wait_recv()

    def project(hf):
        rows = slice(hf * CHUNK, (hf + 1) * CHUNK)
        kv_rows = slice(WIN + hf * CHUNK, WIN + (hf + 1) * CHUNK)

        def kv_step(n, carry):
            off = pl.multiple_of(n * kvd, kvd)
            wcols = pl.ds(pl.multiple_of(d_model + n * kvd, kvd), kvd)
            kvb[kv_rows, pl.ds(off, kvd)] = mm(xg[rows, :], w_v[:, wcols]).astype(BF)
            return carry

        lax.fori_loop(0, 2, kv_step, 0)
        if hf == 1:
            halo.start()

        def q_proj(n, carry):
            off = pl.ds(pl.multiple_of(n * kvd, kvd), kvd)
            qs[rows, off] = mm(xg[rows, :], w_v[:, off]).astype(BF)
            return carry

        lax.fori_loop(0, d_model // kvd, q_proj, 0)

    halo = pltpu.make_async_remote_copy(
        src_ref=kvb.at[pl.ds(seg, WIN)], dst_ref=kvb.at[pl.ds(0, WIN)],
        send_sem=h_ss.at[0], recv_sem=h_rs.at[0], device_id=next_dev, device_id_type=MESH,
    )
    arrive(1)
    project(1)
    arrive(0)
    project(0)
    halo.wait_recv()

    ones = jnp.ones((WIN + ROWS, HD), BF)

    def att_step(n, carry):
        b = n // KV_HEADS
        g = lax.rem(n, KV_HEADS)
        rows = pl.ds(pl.multiple_of(b * ROWS, ROWS), ROWS)
        keys = pl.ds(pl.multiple_of(b * ROWS, ROWS), WIN + ROWS)
        kg = kvb[keys, pl.ds(pl.multiple_of(g * HD, HD), HD)]
        vg = kvb[keys, pl.ds(pl.multiple_of(kvd + g * HD, HD), HD)]
        va = jnp.concatenate([vg, ones], axis=1)
        mask = bias[b]
        for i in range(GROUPS):
            hcols = pl.ds(pl.multiple_of(g * GROUPS * HD + i * HD, HD), HD)
            s = mm_nt(qs[rows, hcols], kg) + mask
            top = jnp.max(s, axis=1, keepdims=True)
            p = jnp.exp2((s - top) * (SCALE * LOG2E)).astype(BF)
            o = mm(p, va)
            att[rows, hcols] = (o[:, :HD] / o[:, HD:]).astype(BF)
        return carry

    lax.fori_loop(0, seg // ROWS * KV_HEADS, att_step, 0)
    att_out = pltpu.make_async_copy(att, att_hbm, out_sem.at[1])
    att_out.start()

    core_cp.wait_send()
    for cp in x_cps + y_cps:
        cp.wait_send()
    for hf in range(2):
        for k in range(1, N_HEAD):
            z_copy(hf, k, lax.rem(z + k, N_HEAD)).wait_send()
    halo.wait_send()
    fen_out.wait()
    att_out.wait()


def shards(
    queries, key_rows, value_rows, level_codes, level_coefs, norm_gain, w_query, w_key, w_value,
    lookback,
):
    tok, feat = queries.shape
    levels = level_codes.shape[1]
    d_model = w_query.shape[0]
    kvd = w_key.shape[1]
    seg = tok // N_HEAD
    chunks = tok // CHUNK
    hbm = pl.BlockSpec(memory_space=pltpu.HBM)
    dma = pltpu.SemaphoreType.DMA
    return pl.pallas_call(
        body,
        out_shape=(
            jax.ShapeDtypeStruct((tok, feat), BF),
            jax.ShapeDtypeStruct((seg, d_model), BF),
        ),
        in_specs=[hbm] * 10,
        out_specs=(hbm, hbm),
        scratch_shapes=[
            pltpu.VMEM((tok, feat), BF),
            pltpu.VMEM((tok, feat), BF),
            pltpu.VMEM((tok, feat), BF),
            pltpu.VMEM((feat, tok), BF),
            pltpu.VMEM((feat, tok), BF),
            pltpu.VMEM((levels, tok), jnp.int32),
            pltpu.SMEM((HERE, NCOEF), F32),
            pltpu.VMEM((HERE, HD), F32),
            pltpu.VMEM((feat, HD), F32),
            pltpu.VMEM((seg // ROWS, ROWS), jnp.int32),
            pltpu.VMEM((HERE, levels, tok), F32),
            pltpu.VMEM((HALF, HALF), jnp.int32),
            pltpu.VMEM((feat, tok), F32),
            pltpu.VMEM((chunks, feat, HD), F32),
            pltpu.VMEM((7, feat, HD), BF),
            pltpu.VMEM((feat, HD), F32),
            pltpu.VMEM((feat, HD), BF),
            pltpu.VMEM((feat, HD), BF),
            pltpu.VMEM((SIDE, feat // 2, HD), BF),
            pltpu.VMEM((SIDE, feat // 2, HD), BF),
            pltpu.VMEM((feat, FAR * HD), BF),
            pltpu.VMEM((tok, feat), BF),
            pltpu.VMEM((seg, d_model), BF),
            pltpu.VMEM((d_model, d_model + 2 * kvd), BF),
            pltpu.VMEM((seg, d_model), BF),
            pltpu.VMEM((seg + WIN, 2 * kvd), BF),
            pltpu.VMEM((seg // ROWS, ROWS, WIN + ROWS), F32),
            pltpu.VMEM((seg, d_model), BF),
            dma((3, 2)), dma((3,)), dma((2,)), dma((4,)),
            dma((1,)), dma((1,)), dma((SIDE,)), dma((SIDE,)), dma((SIDE,)), dma((SIDE,)),
            dma((2,)), dma((2,)), dma((2, N_HEAD)), dma((2, N_HEAD)), dma((1,)), dma((1,)),
        ],
        compiler_params=pltpu.CompilerParams(
            collective_id=0, has_side_effects=True, vmem_limit_bytes=60 << 20
        ),
    )(
        queries, key_rows, value_rows, level_codes.T, level_coefs,
        norm_gain.reshape(HERE, HD), w_query, w_key, w_value, lookback.reshape(seg // ROWS, ROWS),
    )


def solution(mesh):
    in_specs = (
        P("ctx", "head"),
        P("ctx", "head"),
        P("ctx", "head"),
        P("ctx", None),
        P("head", None),
        P("head"),
        P(),
        P(),
        P(),
        P(("ctx", "head")),
    )
    out_specs = (P("ctx", "head"), P(("ctx", "head"), None))
    return jax.shard_map(shards, mesh=mesh, in_specs=in_specs, out_specs=out_specs, check_vma=False)
```

```python
import functools

import jax
import jax.numpy as jnp
from jax import lax
from jax.experimental import pallas as pl
from jax.experimental.pallas import tpu as pltpu
from jax.sharding import PartitionSpec as P

HD = 128
HEADS = 16
KV_HEADS = 4
GROUPS = HEADS // KV_HEADS
WIN = 256
NCOEF = 16
N_HEAD = 4
SIDE = 4
FAR = 5
HERE = HEADS // N_HEAD
CHUNK = 256
HALF = CHUNK // 2
ROWS = 128
NEAR_BITS = 8
MESH = pl.DeviceIdType.MESH
BF = jnp.bfloat16
F32 = jnp.float32
SCALE = HD ** (-0.5)
THROTTLE = True
LOG2E = 1.4426950408889634


def mm(a, b):
    return jnp.dot(a, b, preferred_element_type=F32)


def mm_nt(a, b):
    return lax.dot_general(a, b, (((1,), (1,)), ((), ())), preferred_element_type=F32)


def body(
    q_hbm, k_hbm, v_hbm, codes_hbm, coef_hbm, gain_hbm, wq_hbm, wk_hbm, wv_hbm, look_hbm,
    fen_hbm, att_hbm,
    q_v, k_v, v_v, qt, vt, codes, coef, gain, gain_t, look, lam, lev, loc, cst, lst,
    tot, totb, crecv, xr, yr, far, fen, xg, w_v, qs, kvb, bias, att, relay, part,
    in_sem, w_sem, out_sem, small_sem,
    core_ss, core_rs, x_ss, x_rs, y_ss, y_rs, f_ss, f_rs, z_ss, z_rs, h_ss, h_rs, r_ss, r_rs,
):
    tok = q_hbm.shape[0]
    chunks = tok // CHUNK
    seg = tok // N_HEAD
    d_model = wq_hbm.shape[0]
    kvd = wk_hbm.shape[1]
    feat = HERE * HD
    n_ctx = lax.axis_size("ctx")

    c = lax.axis_index("ctx")
    z = lax.axis_index("head")
    core = lax.rem(c, 2)
    cx = lax.rem(c // 2, SIDE)
    cy = c // (2 * SIDE)
    shard = c * N_HEAD + z

    def at_x(v):
        return (cy * 2 * SIDE + v * 2 + core, z)

    def at_y(v):
        return (v * 2 * SIDE + cx * 2 + core, z)

    def at_z(v):
        return (c, v)

    other_core = (c + 1 - 2 * core, z)
    nshard = n_ctx * N_HEAD
    nxt = lax.rem(shard + 1, nshard)
    prv = lax.rem(shard + nshard - 1, nshard)
    next_dev = (nxt // N_HEAD, lax.rem(nxt, N_HEAD))
    prev_dev = (prv // N_HEAD, lax.rem(prv, N_HEAD))

    barrier = pltpu.get_barrier_semaphore()
    friends = [other_core, next_dev, prev_dev]
    for s in range(1, SIDE):
        friends.append(at_x(lax.rem(cx + s, SIDE)))
        friends.append(at_y(lax.rem(cy + s, SIDE)))
        friends.append(at_z(lax.rem(z + s, N_HEAD)))
    for dev in friends:
        pl.semaphore_signal(barrier, inc=1, device_id=dev, device_id_type=MESH)

    half_tok = tok // 2
    first = []
    for n in range(2):
        rows = pl.ds(n * half_tok, half_tok)
        pair = []
        for a, (src, dst) in enumerate(((v_hbm, v_v), (k_hbm, k_v))):
            cp = pltpu.make_async_copy(src.at[rows], dst.at[rows], in_sem.at[n, a])
            cp.start()
            pair.append(cp)
        first.append(pair)
    small = []
    for a, (src, dst) in enumerate(
        ((codes_hbm, codes), (coef_hbm, coef), (gain_hbm, gain), (look_hbm, look))
    ):
        cp = pltpu.make_async_copy(src, dst, small_sem.at[a])
        cp.start()
        small.append(cp)
    q_in = pltpu.make_async_copy(q_hbm, q_v, in_sem.at[2, 0])
    q_in.start()
    w_in = [
        pltpu.make_async_copy(wk_hbm, w_v.at[:, pl.ds(d_model, kvd)], w_sem.at[0]),
        pltpu.make_async_copy(wv_hbm, w_v.at[:, pl.ds(d_model + kvd, kvd)], w_sem.at[1]),
        pltpu.make_async_copy(wq_hbm, w_v.at[:, pl.ds(0, d_model)], w_sem.at[2]),
    ]
    for cp in w_in:
        cp.start()

    for n in range(2):
        for cp in first[n]:
            cp.wait()

        def state_step(i, carry, n=n):
            start = pl.multiple_of(i * CHUNK, CHUNK)
            rows = pl.ds(start, CHUNK)
            vtc = v_v[rows, :].T
            vt[:, rows] = vtc
            for h in range(HERE):
                hs = slice(h * HD, (h + 1) * HD)
                cst[i, hs, :] = mm(vtc[hs, :], k_v[rows, hs])
            return carry

        lax.fori_loop(n * chunks // 2, (n + 1) * chunks // 2, state_step, 0)

    pairs = [cst[2 * j] + cst[2 * j + 1] for j in range(4)]
    lo4 = pairs[0] + pairs[1]
    total = lo4 + (pairs[2] + pairs[3])
    tot[...] = total
    totb[...] = total.astype(BF)
    for j in range(4):
        lst[j] = cst[2 * j].astype(BF)
    lst[4] = pairs[0].astype(BF)
    lst[5] = pairs[2].astype(BF)
    lst[6] = lo4.astype(BF)

    pl.semaphore_wait(barrier, len(friends))
    core_cp = pltpu.make_async_remote_copy(
        src_ref=totb, dst_ref=crecv, send_sem=core_ss.at[0], recv_sem=core_rs.at[0],
        device_id=other_core, device_id_type=MESH,
    )
    core_cp.start()

    for cp in small:
        cp.wait()
    si = lax.broadcasted_iota(jnp.int32, (HALF, HALF), 0)
    ti = lax.broadcasted_iota(jnp.int32, (HALF, HALF), 1)
    diff = jnp.bitwise_xor(si, ti)
    level = jnp.zeros((HALF, HALF), jnp.int32)
    for b in range(NEAR_BITS - 1):
        level = level + jnp.where(diff >= (1 << b), 1, 0)
    lev[...] = jnp.where(si <= ti, level, 99)
    for h in range(HERE):
        gain_t[h * HD : (h + 1) * HD, :] = jnp.broadcast_to(gain[h : h + 1, :], (HD, HD)).T

    my_half = pl.multiple_of(core * (feat // 2), feat // 2)
    half_rows = pl.ds(my_half, feat // 2)

    core_cp.wait_recv()
    xr[cx] = (tot[half_rows, :] + crecv[half_rows, :].astype(F32)).astype(BF)
    x_cps = []
    for s in (2, 1, 3):
        cp = pltpu.make_async_remote_copy(
            src_ref=xr.at[cx], dst_ref=xr.at[cx], send_sem=x_ss.at[s], recv_sem=x_rs.at[s],
            device_id=at_x(lax.rem(cx + s, SIDE)), device_id_type=MESH,
        )
        cp.start()
        x_cps.append(cp)
    far[:, 0:HD] = jnp.where(core == 1, crecv[...].astype(F32), 0.0).astype(BF)

    def lam_step(i, carry):
        cols = pl.ds(pl.multiple_of(i * CHUNK, CHUNK), CHUNK)
        cd = codes[:, cols]
        for h in range(HERE):
            acc = jnp.full(cd.shape, coef[h, 0], F32)
            for n in range(1, NCOEF):
                acc = jnp.where(cd == n, coef[h, n], acc)
            lam[h, :, cols] = acc
        return carry

    lax.fori_loop(0, chunks, lam_step, 0)
    q_in.wait()

    def q_step(i, carry):
        rows = pl.ds(pl.multiple_of(i * CHUNK, CHUNK), CHUNK)
        qt[:, rows] = q_v[rows, :].T
        return carry

    lax.fori_loop(0, chunks, q_step, 0)

    def local_chunk(i):
        t0 = i * CHUNK
        cols = slice(t0, t0 + CHUNK)

        def head(h, carry):
            hoff = pl.multiple_of(h * HD, HD)
            hrows = pl.ds(hoff, HD)
            qth = qt[hrows, cols]
            st = mm(k_v[cols, hrows], qth)
            lamh = lam.at[h]

            def quad(a):
                lo = t0 + a * HALF
                w = jnp.zeros((HALF, HALF), F32)
                lv = lev[...]
                for l in range(NEAR_BITS):
                    w = jnp.where(lv == l, lamh[l : l + 1, lo : lo + HALF], w)
                return (st[a * HALF : (a + 1) * HALF, a * HALF : (a + 1) * HALF] * w).astype(BF)

            cross = (
                st[:HALF, HALF:] * lamh[NEAR_BITS : NEAR_BITS + 1, t0 + HALF : t0 + CHUNK]
            ).astype(BF)
            top = jnp.concatenate([quad(0), cross], axis=1)
            low = jnp.concatenate([jnp.zeros((HALF, HALF), BF), quad(1)], axis=1)
            terms = jnp.concatenate([top, low], axis=0)
            acc = mm(vt[hrows, cols], terms)
            used = []
            if i & 1:
                used.append((i // 2, 9))
            if i & 2:
                used.append((4 + i // 4, 10))
            if i & 4:
                used.append((6, 11))
            for slot, l in used:
                ql = qth * jnp.broadcast_to(lamh[l : l + 1, cols], (HD, CHUNK)).astype(BF)
                acc = acc + mm(lst[slot, hrows, :], ql)
            loc[hrows, cols] = acc
            return carry

        lax.fori_loop(0, HERE, head, 0)

    for i in (7, 6):
        local_chunk(i)

    for cp in x_cps:
        cp.wait_recv()

    def m(cond):
        return jnp.where(cond, 1.0, 0.0).astype(F32)

    def level_pair(buf, pos):
        parts = [buf[j].astype(F32) for j in range(SIDE)]
        low = parts[0] + parts[1]
        one = parts[0] * m(pos == 1) + parts[2] * m(pos == 3)
        two = low * m(pos >= 2)
        return one.astype(BF), two.astype(BF), low + (parts[2] + parts[3])

    one, two, row_sum = level_pair(xr, cx)
    yr[cy] = row_sum.astype(BF)
    y_cps = []
    for s in (2, 1, 3):
        cp = pltpu.make_async_remote_copy(
            src_ref=yr.at[cy], dst_ref=yr.at[cy], send_sem=y_ss.at[s], recv_sem=y_rs.at[s],
            device_id=at_y(lax.rem(cy + s, SIDE)), device_id_type=MESH,
        )
        cp.start()
        y_cps.append(cp)
    far[half_rows, HD : 2 * HD] = one
    far[half_rows, 2 * HD : 3 * HD] = two

    def pass_on(n):
        piece = far.at[half_rows, pl.ds((2 * n + 1) * HD, 2 * HD)]
        cp = pltpu.make_async_remote_copy(
            src_ref=piece, dst_ref=piece, send_sem=f_ss.at[n], recv_sem=f_rs.at[n],
            device_id=other_core, device_id_type=MESH,
        )
        cp.start()
        return cp

    f_cps = [pass_on(0)]

    for i in (5, 4, 3, 2, 1, 0):
        local_chunk(i)

    ri = lax.broadcasted_iota(jnp.int32, (ROWS, WIN + ROWS), 0)
    ji = lax.broadcasted_iota(jnp.int32, (ROWS, WIN + ROWS), 1)
    gap = WIN + ri - ji
    for b in range(seg // ROWS):
        reach = jnp.broadcast_to(look[b : b + 1, :].astype(F32), (ROWS, ROWS)).T
        reach = jnp.concatenate([reach] * 3, axis=1).astype(jnp.int32)
        key_pos = shard * seg + b * ROWS - WIN + ji
        ok = (gap >= 0) & (gap <= reach) & (key_pos >= 0)
        bias[b] = jnp.where(ok, 0.0, -1e30)

    for cp in y_cps:
        cp.wait_recv()
    one, two, _ = level_pair(yr, cy)
    far[half_rows, 3 * HD : 4 * HD] = one
    far[half_rows, 4 * HD : 5 * HD] = two
    f_cps.append(pass_on(1))
    for cp in f_cps:
        cp.wait()

    def chunk_of(n):
        hf = 1 - n // N_HEAD
        j = lax.rem(n, N_HEAD)
        k = jnp.where(j == 0, 2, jnp.where(j == 1, 1, jnp.where(j == 2, 3, 0)))
        dest = lax.rem(z + k, N_HEAD)
        return hf, k, dest

    def z_copy(hf, k, dest):
        src_rows = pl.ds(pl.multiple_of(dest * seg + hf * CHUNK, CHUNK), CHUNK)
        return pltpu.make_async_remote_copy(
            src_ref=fen.at[src_rows],
            dst_ref=xg.at[
                pl.ds(pl.multiple_of(hf * CHUNK, CHUNK), CHUNK),
                pl.ds(pl.multiple_of(z * feat, feat), feat),
            ],
            send_sem=z_ss.at[hf, k],
            recv_sem=z_rs.at[hf, k],
            device_id=at_z(dest),
            device_id_type=MESH,
        )

    def far_step(n, carry):
        hf, k, dest = chunk_of(n)
        start = pl.multiple_of(dest * seg + hf * CHUNK, CHUNK)
        cols = pl.ds(start, CHUNK)
        for h in range(HERE):
            hs = slice(h * HD, (h + 1) * HD)
            qth = qt[hs, cols]
            parts = []
            for l in range(FAR):
                row = lam[h, 12 + l : 13 + l, cols]
                parts.append(qth * jnp.broadcast_to(row, (HD, CHUNK)).astype(BF))
            acc = loc[hs, cols] + mm(far[hs, :], jnp.concatenate(parts, axis=0))
            ms = jnp.sum(acc * acc, axis=0, keepdims=True)
            r = SCALE * lax.rsqrt(ms * (SCALE * SCALE / HD) + 1e-06)
            g = gain_t[hs, :]
            g = jnp.concatenate([g, g], axis=1)
            fen[cols, hs] = (acc * r * g).astype(BF).T

        @pl.when((k > 0) & (hf == 1))
        def _():
            z_copy(1, k, dest).start()

        @pl.when(k == 0)
        def _():
            xg[
                pl.ds(pl.multiple_of(hf * CHUNK, CHUNK), CHUNK),
                pl.ds(pl.multiple_of(z * feat, feat), feat),
            ] = fen[cols, :]

        return carry

    def to_z(k):
        return lax.rem(z + k, N_HEAD)

    lax.fori_loop(0, 2 * N_HEAD, far_step, 0)
    fen_out = pltpu.make_async_copy(fen, fen_hbm, out_sem.at[0])
    fen_out.start()

    if THROTTLE:
        for k in (1, 3, 2):
            z_copy(1, k, to_z(k)).wait_send()
    hop = pltpu.make_async_remote_copy(
        src_ref=fen.at[pl.ds(pl.multiple_of(to_z(2) * seg, CHUNK), CHUNK)],
        dst_ref=relay,
        send_sem=r_ss.at[0], recv_sem=r_rs.at[0],
        device_id=at_z(to_z(3)), device_id_type=MESH,
    )
    hop.start()
    z_copy(0, 1, to_z(1)).start()
    z_copy(0, 3, to_z(3)).start()
    onward = pltpu.make_async_remote_copy(
        src_ref=relay,
        dst_ref=xg.at[pl.ds(0, CHUNK), pl.ds(pl.multiple_of(to_z(1) * feat, feat), feat)],
        send_sem=z_ss.at[0, 2], recv_sem=z_rs.at[0, 2],
        device_id=at_z(to_z(3)), device_id_type=MESH,
    )
    halo = pltpu.make_async_remote_copy(
        src_ref=kvb.at[pl.ds(seg, WIN)], dst_ref=kvb.at[pl.ds(0, WIN)],
        send_sem=h_ss.at[0], recv_sem=h_rs.at[0], device_id=next_dev, device_id_type=MESH,
    )
    for cp in w_in:
        cp.wait()

    for k in (1, 3, 2):
        z_copy(1, k, to_z(k)).wait_recv()
    late = slice(CHUNK, 2 * CHUNK)
    for n in range(2):
        wcols = slice(d_model + n * kvd, d_model + (n + 1) * kvd)
        kvb[WIN + CHUNK :, n * kvd : (n + 1) * kvd] = mm(xg[late, :], w_v[:, wcols]).astype(BF)
    halo.start()

    def q_proj(n, carry):
        off = pl.ds(pl.multiple_of(n * kvd, kvd), kvd)
        qs[late, off] = mm(xg[late, :], w_v[:, off]).astype(BF)
        return carry

    lax.fori_loop(0, d_model // kvd, q_proj, 0)
    hop.wait_recv()
    onward.start()

    def two(j, k, off):
        total = None
        for s in (j, k):
            fs = pl.ds(pl.multiple_of(lax.rem(z + N_HEAD - s, N_HEAD) * feat, feat), feat)
            term = mm(xg[0:CHUNK, fs], w_v[fs, off])
            total = term if total is None else total + term
        return total

    z_copy(0, 1, to_z(1)).wait_recv()

    def part_step(n, carry):
        off = pl.ds(pl.multiple_of(n * kvd, kvd), kvd)
        part[:, off] = two(0, 1, off)
        return carry

    lax.fori_loop(0, d_model // kvd + 2, part_step, 0)
    z_copy(0, 3, to_z(3)).wait_recv()
    onward.wait_recv()
    for n in range(2):
        wcols = pl.ds(d_model + n * kvd, kvd)
        kvb[WIN : WIN + CHUNK, n * kvd : (n + 1) * kvd] = (part[:, wcols] + two(3, 2, wcols)).astype(BF)

    def q_rest(n, carry):
        off = pl.ds(pl.multiple_of(n * kvd, kvd), kvd)
        qs[0:CHUNK, off] = (part[:, off] + two(3, 2, off)).astype(BF)
        return carry

    lax.fori_loop(0, d_model // kvd, q_rest, 0)

    ones = jnp.ones((WIN + ROWS, HD), BF)

    def attend(b, g):
        rows = slice(b * ROWS, (b + 1) * ROWS)
        keys = slice(b * ROWS, b * ROWS + WIN + ROWS)
        kg = kvb[keys, g * HD : (g + 1) * HD]
        vg = kvb[keys, kvd + g * HD : kvd + (g + 1) * HD]
        va = jnp.concatenate([vg, ones], axis=1)
        mask = bias[b]
        for i in range(GROUPS):
            hcols = slice((g * GROUPS + i) * HD, (g * GROUPS + i + 1) * HD)
            s = mm_nt(qs[rows, hcols], kg) + mask
            top = jnp.max(s, axis=1, keepdims=True)
            p = jnp.exp2((s - top) * (SCALE * LOG2E)).astype(BF)
            o = mm(p, va)
            att[rows, hcols] = (o[:, :HD] / o[:, HD:]).astype(BF)

    def att_half(n):
        for b in (2 * n, 2 * n + 1):
            for g in range(KV_HEADS):
                attend(b, g)
        rows = pl.ds(n * CHUNK, CHUNK)
        cp = pltpu.make_async_copy(att.at[rows], att_hbm.at[rows], out_sem.at[1 + n])
        cp.start()
        return cp

    att_out = [att_half(1)]
    halo.wait_recv()
    att_out.append(att_half(0))

    core_cp.wait_send()
    for cp in x_cps + y_cps:
        cp.wait_send()
    if not THROTTLE:
        for k in (1, 3, 2):
            z_copy(1, k, to_z(k)).wait_send()
    z_copy(0, 1, to_z(1)).wait_send()
    z_copy(0, 3, to_z(3)).wait_send()
    hop.wait_send()
    onward.wait_send()
    halo.wait_send()
    fen_out.wait()
    for cp in att_out:
        cp.wait()


def shards(
    queries, key_rows, value_rows, level_codes, level_coefs, norm_gain, w_query, w_key, w_value,
    lookback,
):
    tok, feat = queries.shape
    levels = level_codes.shape[1]
    d_model = w_query.shape[0]
    kvd = w_key.shape[1]
    seg = tok // N_HEAD
    chunks = tok // CHUNK
    hbm = pl.BlockSpec(memory_space=pltpu.HBM)
    dma = pltpu.SemaphoreType.DMA
    return pl.pallas_call(
        body,
        out_shape=(
            jax.ShapeDtypeStruct((tok, feat), BF),
            jax.ShapeDtypeStruct((seg, d_model), BF),
        ),
        in_specs=[hbm] * 10,
        out_specs=(hbm, hbm),
        scratch_shapes=[
            pltpu.VMEM((tok, feat), BF),
            pltpu.VMEM((tok, feat), BF),
            pltpu.VMEM((tok, feat), BF),
            pltpu.VMEM((feat, tok), BF),
            pltpu.VMEM((feat, tok), BF),
            pltpu.VMEM((levels, tok), jnp.int32),
            pltpu.SMEM((HERE, NCOEF), F32),
            pltpu.VMEM((HERE, HD), F32),
            pltpu.VMEM((feat, HD), F32),
            pltpu.VMEM((seg // ROWS, ROWS), jnp.int32),
            pltpu.VMEM((HERE, levels, tok), F32),
            pltpu.VMEM((HALF, HALF), jnp.int32),
            pltpu.VMEM((feat, tok), F32),
            pltpu.VMEM((chunks, feat, HD), F32),
            pltpu.VMEM((7, feat, HD), BF),
            pltpu.VMEM((feat, HD), F32),
            pltpu.VMEM((feat, HD), BF),
            pltpu.VMEM((feat, HD), BF),
            pltpu.VMEM((SIDE, feat // 2, HD), BF),
            pltpu.VMEM((SIDE, feat // 2, HD), BF),
            pltpu.VMEM((feat, FAR * HD), BF),
            pltpu.VMEM((tok, feat), BF),
            pltpu.VMEM((seg, d_model), BF),
            pltpu.VMEM((d_model, d_model + 2 * kvd), BF),
            pltpu.VMEM((seg, d_model), BF),
            pltpu.VMEM((seg + WIN, 2 * kvd), BF),
            pltpu.VMEM((seg // ROWS, ROWS, WIN + ROWS), F32),
            pltpu.VMEM((seg, d_model), BF),
            pltpu.VMEM((CHUNK, feat), BF),
            pltpu.VMEM((CHUNK, d_model + 2 * kvd), F32),
            dma((3, 2)), dma((3,)), dma((3,)), dma((4,)),
            dma((1,)), dma((1,)), dma((SIDE,)), dma((SIDE,)), dma((SIDE,)), dma((SIDE,)),
            dma((2,)), dma((2,)), dma((2, N_HEAD)), dma((2, N_HEAD)), dma((1,)), dma((1,)),
            dma((1,)), dma((1,)),
        ],
        compiler_params=pltpu.CompilerParams(
            collective_id=0, has_side_effects=True, vmem_limit_bytes=60 << 20
        ),
    )(
        queries, key_rows, value_rows, level_codes.T, level_coefs,
        norm_gain.reshape(HERE, HD), w_query, w_key, w_value, lookback.reshape(seg // ROWS, ROWS),
    )


def solution(mesh):
    in_specs = (
        P("ctx", "head"),
        P("ctx", "head"),
        P("ctx", "head"),
        P("ctx", None),
        P("head", None),
        P("head"),
        P(),
        P(),
        P(),
        P(("ctx", "head")),
    )
    out_specs = (P("ctx", "head"), P(("ctx", "head"), None))
    return jax.shard_map(shards, mesh=mesh, in_specs=in_specs, out_specs=out_specs, check_vma=False)
```

```python
import functools

import jax
import jax.numpy as jnp
from jax import lax
from jax.experimental import pallas as pl
from jax.experimental.pallas import tpu as pltpu
from jax.sharding import PartitionSpec as P

HD = 128
HEADS = 16
KV_HEADS = 4
GROUPS = HEADS // KV_HEADS
WIN = 256
NCOEF = 16
N_HEAD = 4
SIDE = 4
FAR = 5
HERE = HEADS // N_HEAD
CHUNK = 256
HALF = CHUNK // 2
ROWS = 128
NEAR_BITS = 8
MESH = pl.DeviceIdType.MESH
BF = jnp.bfloat16
F32 = jnp.float32
SCALE = HD ** (-0.5)
THROTTLE = True
LOG2E = 1.4426950408889634


def mm(a, b):
    return jnp.dot(a, b, preferred_element_type=F32)


def mm_nt(a, b):
    return lax.dot_general(a, b, (((1,), (1,)), ((), ())), preferred_element_type=F32)


def body(
    q_hbm, k_hbm, v_hbm, codes_hbm, coef_hbm, gain_hbm, wq_hbm, wk_hbm, wv_hbm, look_hbm,
    fen, qs, kvb, bias,
    q_v, k_v, v_v, qt, vt, codes, coef, gain, gain_t, look, lam, lev, loc, cst, lst,
    tot, totb, crecv, xr, yr, far, xg, w_v, relay, part,
    in_sem, w_sem, small_sem,
    core_ss, core_rs, x_ss, x_rs, y_ss, y_rs, f_ss, f_rs, z_ss, z_rs, h_ss, h_rs, r_ss, r_rs,
):
    tok = q_hbm.shape[0]
    chunks = tok // CHUNK
    seg = tok // N_HEAD
    d_model = wq_hbm.shape[0]
    kvd = wk_hbm.shape[1]
    feat = HERE * HD
    n_ctx = lax.axis_size("ctx")

    c = lax.axis_index("ctx")
    z = lax.axis_index("head")
    core = lax.rem(c, 2)
    cx = lax.rem(c // 2, SIDE)
    cy = c // (2 * SIDE)
    shard = c * N_HEAD + z

    def at_x(v):
        return (cy * 2 * SIDE + v * 2 + core, z)

    def at_y(v):
        return (v * 2 * SIDE + cx * 2 + core, z)

    def at_z(v):
        return (c, v)

    other_core = (c + 1 - 2 * core, z)
    nshard = n_ctx * N_HEAD
    nxt = lax.rem(shard + 1, nshard)
    prv = lax.rem(shard + nshard - 1, nshard)
    next_dev = (nxt // N_HEAD, lax.rem(nxt, N_HEAD))
    prev_dev = (prv // N_HEAD, lax.rem(prv, N_HEAD))

    barrier = pltpu.get_barrier_semaphore()
    friends = [other_core, next_dev, prev_dev]
    for s in range(1, SIDE):
        friends.append(at_x(lax.rem(cx + s, SIDE)))
        friends.append(at_y(lax.rem(cy + s, SIDE)))
        friends.append(at_z(lax.rem(z + s, N_HEAD)))
    for dev in friends:
        pl.semaphore_signal(barrier, inc=1, device_id=dev, device_id_type=MESH)

    quarter = tok // 4
    first = []
    for n in range(4):
        rows = pl.ds(n * quarter, quarter)
        pair = []
        for a, (src, dst) in enumerate(((v_hbm, v_v), (k_hbm, k_v))):
            cp = pltpu.make_async_copy(src.at[rows], dst.at[rows], in_sem.at[n, a])
            cp.start()
            pair.append(cp)
        first.append(pair)
    small = []
    for a, (src, dst) in enumerate(
        ((codes_hbm, codes), (coef_hbm, coef), (gain_hbm, gain), (look_hbm, look))
    ):
        cp = pltpu.make_async_copy(src, dst, small_sem.at[a])
        cp.start()
        small.append(cp)
    q_in = pltpu.make_async_copy(q_hbm, q_v, in_sem.at[4, 0])
    q_in.start()
    w_in = [
        pltpu.make_async_copy(wk_hbm, w_v.at[:, pl.ds(d_model, kvd)], w_sem.at[0]),
        pltpu.make_async_copy(wv_hbm, w_v.at[:, pl.ds(d_model + kvd, kvd)], w_sem.at[1]),
        pltpu.make_async_copy(wq_hbm, w_v.at[:, pl.ds(0, d_model)], w_sem.at[2]),
    ]
    for cp in w_in:
        cp.start()

    for n in range(4):
        for cp in first[n]:
            cp.wait()

        def state_step(i, carry, n=n):
            start = pl.multiple_of(i * CHUNK, CHUNK)
            rows = pl.ds(start, CHUNK)
            vtc = v_v[rows, :].T
            vt[:, rows] = vtc
            for h in range(HERE):
                hs = slice(h * HD, (h + 1) * HD)
                cst[i, hs, :] = mm(vtc[hs, :], k_v[rows, hs])
            return carry

        lax.fori_loop(n * chunks // 4, (n + 1) * chunks // 4, state_step, 0)

    pairs = [cst[2 * j] + cst[2 * j + 1] for j in range(4)]
    lo4 = pairs[0] + pairs[1]
    total = lo4 + (pairs[2] + pairs[3])
    tot[...] = total
    totb[...] = total.astype(BF)
    for j in range(4):
        lst[j] = cst[2 * j].astype(BF)
    lst[4] = pairs[0].astype(BF)
    lst[5] = pairs[2].astype(BF)
    lst[6] = lo4.astype(BF)

    pl.semaphore_wait(barrier, len(friends))
    core_cp = pltpu.make_async_remote_copy(
        src_ref=totb, dst_ref=crecv, send_sem=core_ss.at[0], recv_sem=core_rs.at[0],
        device_id=other_core, device_id_type=MESH,
    )
    core_cp.start()

    for cp in small:
        cp.wait()
    si = lax.broadcasted_iota(jnp.int32, (HALF, HALF), 0)
    ti = lax.broadcasted_iota(jnp.int32, (HALF, HALF), 1)
    diff = jnp.bitwise_xor(si, ti)
    level = jnp.zeros((HALF, HALF), jnp.int32)
    for b in range(NEAR_BITS - 1):
        level = level + jnp.where(diff >= (1 << b), 1, 0)
    lev[...] = jnp.where(si <= ti, level, 99)
    for h in range(HERE):
        gain_t[h * HD : (h + 1) * HD, :] = jnp.broadcast_to(gain[h : h + 1, :], (HD, HD)).T

    my_half = pl.multiple_of(core * (feat // 2), feat // 2)
    half_rows = pl.ds(my_half, feat // 2)

    core_cp.wait_recv()
    xr[cx] = (tot[half_rows, :] + crecv[half_rows, :].astype(F32)).astype(BF)
    x_cps = []
    for s in (2, 1, 3):
        cp = pltpu.make_async_remote_copy(
            src_ref=xr.at[cx], dst_ref=xr.at[cx], send_sem=x_ss.at[s], recv_sem=x_rs.at[s],
            device_id=at_x(lax.rem(cx + s, SIDE)), device_id_type=MESH,
        )
        cp.start()
        x_cps.append(cp)
    far[:, 0:HD] = jnp.where(core == 1, crecv[...].astype(F32), 0.0).astype(BF)

    def lam_step(i, carry):
        cols = pl.ds(pl.multiple_of(i * CHUNK, CHUNK), CHUNK)
        cd = codes[:, cols]
        for h in range(HERE):
            acc = jnp.full(cd.shape, coef[h, 0], F32)
            for n in range(1, NCOEF):
                acc = jnp.where(cd == n, coef[h, n], acc)
            lam[h, :, cols] = acc
        return carry

    lax.fori_loop(0, chunks, lam_step, 0)
    q_in.wait()

    def q_step(i, carry):
        rows = pl.ds(pl.multiple_of(i * CHUNK, CHUNK), CHUNK)
        qt[:, rows] = q_v[rows, :].T
        return carry

    lax.fori_loop(0, chunks, q_step, 0)

    def local_chunk(i):
        t0 = i * CHUNK
        cols = slice(t0, t0 + CHUNK)

        def head(h, carry):
            hoff = pl.multiple_of(h * HD, HD)
            hrows = pl.ds(hoff, HD)
            qth = qt[hrows, cols]
            st = mm(k_v[cols, hrows], qth)
            lamh = lam.at[h]

            def quad(a):
                lo = t0 + a * HALF
                w = jnp.zeros((HALF, HALF), F32)
                lv = lev[...]
                for l in range(NEAR_BITS):
                    w = jnp.where(lv == l, lamh[l : l + 1, lo : lo + HALF], w)
                return (st[a * HALF : (a + 1) * HALF, a * HALF : (a + 1) * HALF] * w).astype(BF)

            cross = (
                st[:HALF, HALF:] * lamh[NEAR_BITS : NEAR_BITS + 1, t0 + HALF : t0 + CHUNK]
            ).astype(BF)
            top = jnp.concatenate([quad(0), cross], axis=1)
            low = jnp.concatenate([jnp.zeros((HALF, HALF), BF), quad(1)], axis=1)
            terms = jnp.concatenate([top, low], axis=0)
            acc = mm(vt[hrows, cols], terms)
            used = []
            if i & 1:
                used.append((i // 2, 9))
            if i & 2:
                used.append((4 + i // 4, 10))
            if i & 4:
                used.append((6, 11))
            for slot, l in used:
                ql = qth * jnp.broadcast_to(lamh[l : l + 1, cols], (HD, CHUNK)).astype(BF)
                acc = acc + mm(lst[slot, hrows, :], ql)
            loc[hrows, cols] = acc
            return carry

        lax.fori_loop(0, HERE, head, 0)

    for i in (7, 5):
        local_chunk(i)

    for cp in x_cps:
        cp.wait_recv()

    def m(cond):
        return jnp.where(cond, 1.0, 0.0).astype(F32)

    def level_pair(buf, pos):
        parts = [buf[j].astype(F32) for j in range(SIDE)]
        low = parts[0] + parts[1]
        one = parts[0] * m(pos == 1) + parts[2] * m(pos == 3)
        two = low * m(pos >= 2)
        return one.astype(BF), two.astype(BF), low + (parts[2] + parts[3])

    one, two, row_sum = level_pair(xr, cx)
    yr[cy] = row_sum.astype(BF)
    y_cps = []
    for s in (2, 1, 3):
        cp = pltpu.make_async_remote_copy(
            src_ref=yr.at[cy], dst_ref=yr.at[cy], send_sem=y_ss.at[s], recv_sem=y_rs.at[s],
            device_id=at_y(lax.rem(cy + s, SIDE)), device_id_type=MESH,
        )
        cp.start()
        y_cps.append(cp)
    far[half_rows, HD : 2 * HD] = one
    far[half_rows, 2 * HD : 3 * HD] = two

    def pass_on(n):
        piece = far.at[half_rows, pl.ds((2 * n + 1) * HD, 2 * HD)]
        cp = pltpu.make_async_remote_copy(
            src_ref=piece, dst_ref=piece, send_sem=f_ss.at[n], recv_sem=f_rs.at[n],
            device_id=other_core, device_id_type=MESH,
        )
        cp.start()
        return cp

    f_cps = [pass_on(0)]

    for i in (3, 1):
        local_chunk(i)

    for cp in y_cps:
        cp.wait_recv()
    one, two, _ = level_pair(yr, cy)
    far[half_rows, 3 * HD : 4 * HD] = one
    far[half_rows, 4 * HD : 5 * HD] = two
    f_cps.append(pass_on(1))
    for cp in f_cps:
        cp.wait()

    def chunk_of(n):
        hf = 1 - n // N_HEAD
        j = lax.rem(n, N_HEAD)
        k = jnp.where(j == 0, 2, jnp.where(j == 1, 1, jnp.where(j == 2, 3, 0)))
        dest = lax.rem(z + k, N_HEAD)
        return hf, k, dest

    def z_copy(hf, k, dest):
        src_rows = pl.ds(pl.multiple_of(dest * seg + hf * CHUNK, CHUNK), CHUNK)
        return pltpu.make_async_remote_copy(
            src_ref=fen.at[src_rows],
            dst_ref=xg.at[
                pl.ds(pl.multiple_of(hf * CHUNK, CHUNK), CHUNK),
                pl.ds(pl.multiple_of(z * feat, feat), feat),
            ],
            send_sem=z_ss.at[hf, k],
            recv_sem=z_rs.at[hf, k],
            device_id=at_z(dest),
            device_id_type=MESH,
        )

    def far_step(n, carry):
        hf, k, dest = chunk_of(n)
        start = pl.multiple_of(dest * seg + hf * CHUNK, CHUNK)
        cols = pl.ds(start, CHUNK)
        for h in range(HERE):
            hs = slice(h * HD, (h + 1) * HD)
            qth = qt[hs, cols]
            parts = []
            for l in range(FAR):
                row = lam[h, 12 + l : 13 + l, cols]
                parts.append(qth * jnp.broadcast_to(row, (HD, CHUNK)).astype(BF))
            acc = loc[hs, cols] + mm(far[hs, :], jnp.concatenate(parts, axis=0))
            ms = jnp.sum(acc * acc, axis=0, keepdims=True)
            r = SCALE * lax.rsqrt(ms * (SCALE * SCALE / HD) + 1e-06)
            g = gain_t[hs, :]
            g = jnp.concatenate([g, g], axis=1)
            fen[cols, hs] = (acc * r * g).astype(BF).T

        @pl.when((k > 0) & (hf == 1))
        def _():
            z_copy(1, k, dest).start()

        @pl.when(k == 0)
        def _():
            xg[
                pl.ds(pl.multiple_of(hf * CHUNK, CHUNK), CHUNK),
                pl.ds(pl.multiple_of(z * feat, feat), feat),
            ] = fen[cols, :]

        return carry

    def to_z(k):
        return lax.rem(z + k, N_HEAD)

    lax.fori_loop(0, N_HEAD, far_step, 0)
    for i in (6, 4, 2, 0):
        local_chunk(i)
    lax.fori_loop(N_HEAD, 2 * N_HEAD, far_step, 0)

    ri = lax.broadcasted_iota(jnp.int32, (ROWS, WIN + ROWS), 0)
    ji = lax.broadcasted_iota(jnp.int32, (ROWS, WIN + ROWS), 1)
    gap = WIN + ri - ji
    for b in range(seg // ROWS):
        reach = jnp.broadcast_to(look[b : b + 1, :].astype(F32), (ROWS, ROWS)).T
        reach = jnp.concatenate([reach] * 3, axis=1).astype(jnp.int32)
        key_pos = shard * seg + b * ROWS - WIN + ji
        ok = (gap >= 0) & (gap <= reach) & (key_pos >= 0)
        bias[b] = jnp.where(ok, 0.0, -1e30)

    if THROTTLE:
        for k in (1, 3, 2):
            z_copy(1, k, to_z(k)).wait_send()
    hop = pltpu.make_async_remote_copy(
        src_ref=fen.at[pl.ds(pl.multiple_of(to_z(2) * seg, CHUNK), CHUNK)],
        dst_ref=relay,
        send_sem=r_ss.at[0], recv_sem=r_rs.at[0],
        device_id=at_z(to_z(3)), device_id_type=MESH,
    )
    hop.start()
    z_copy(0, 1, to_z(1)).start()
    z_copy(0, 3, to_z(3)).start()
    onward = pltpu.make_async_remote_copy(
        src_ref=relay,
        dst_ref=xg.at[pl.ds(0, CHUNK), pl.ds(pl.multiple_of(to_z(1) * feat, feat), feat)],
        send_sem=z_ss.at[0, 2], recv_sem=z_rs.at[0, 2],
        device_id=at_z(to_z(3)), device_id_type=MESH,
    )
    halo = pltpu.make_async_remote_copy(
        src_ref=kvb.at[pl.ds(seg, WIN)], dst_ref=kvb.at[pl.ds(0, WIN)],
        send_sem=h_ss.at[0], recv_sem=h_rs.at[0], device_id=next_dev, device_id_type=MESH,
    )
    for cp in w_in:
        cp.wait()

    for k in (1, 3, 2):
        z_copy(1, k, to_z(k)).wait_recv()
    late = slice(CHUNK, 2 * CHUNK)
    for n in range(2):
        wcols = slice(d_model + n * kvd, d_model + (n + 1) * kvd)
        kvb[WIN + CHUNK :, n * kvd : (n + 1) * kvd] = mm(xg[late, :], w_v[:, wcols]).astype(BF)
    halo.start()

    def q_proj(n, carry):
        off = pl.ds(pl.multiple_of(n * kvd, kvd), kvd)
        qs[late, off] = mm(xg[late, :], w_v[:, off]).astype(BF)
        return carry

    lax.fori_loop(0, d_model // kvd, q_proj, 0)
    hop.wait_recv()
    onward.start()

    def two(j, k, off):
        total = None
        for s in (j, k):
            fs = pl.ds(pl.multiple_of(lax.rem(z + N_HEAD - s, N_HEAD) * feat, feat), feat)
            term = mm(xg[0:CHUNK, fs], w_v[fs, off])
            total = term if total is None else total + term
        return total

    z_copy(0, 1, to_z(1)).wait_recv()

    def part_step(n, carry):
        off = pl.ds(pl.multiple_of(n * kvd, kvd), kvd)
        part[:, off] = two(0, 1, off)
        return carry

    lax.fori_loop(0, d_model // kvd + 2, part_step, 0)
    z_copy(0, 3, to_z(3)).wait_recv()
    onward.wait_recv()
    for n in range(2):
        wcols = pl.ds(d_model + n * kvd, kvd)
        kvb[WIN : WIN + CHUNK, n * kvd : (n + 1) * kvd] = (part[:, wcols] + two(3, 2, wcols)).astype(BF)

    def q_rest(n, carry):
        off = pl.ds(pl.multiple_of(n * kvd, kvd), kvd)
        qs[0:CHUNK, off] = (part[:, off] + two(3, 2, off)).astype(BF)
        return carry

    lax.fori_loop(0, d_model // kvd, q_rest, 0)

    halo.wait_recv()
    core_cp.wait_send()
    for cp in x_cps + y_cps:
        cp.wait_send()
    if not THROTTLE:
        for k in (1, 3, 2):
            z_copy(1, k, to_z(k)).wait_send()
    z_copy(0, 1, to_z(1)).wait_send()
    z_copy(0, 3, to_z(3)).wait_send()
    hop.wait_send()
    onward.wait_send()
    halo.wait_send()


def attention(fen, qs, kvb, bias, fen_hbm, att_hbm, att, out_sem):
    kvd = kvb.shape[1] // 2
    fen_out = pltpu.make_async_copy(fen, fen_hbm, out_sem.at[0])
    fen_out.start()
    ones = jnp.ones((WIN + ROWS, HD), BF)

    def attend(b, g):
        rows = slice(b * ROWS, (b + 1) * ROWS)
        keys = slice(b * ROWS, b * ROWS + WIN + ROWS)
        kg = kvb[keys, g * HD : (g + 1) * HD]
        vg = kvb[keys, kvd + g * HD : kvd + (g + 1) * HD]
        va = jnp.concatenate([vg, ones], axis=1)
        mask = bias[b]
        for i in range(GROUPS):
            hcols = slice((g * GROUPS + i) * HD, (g * GROUPS + i + 1) * HD)
            s = mm_nt(qs[rows, hcols], kg) + mask
            top = jnp.max(s, axis=1, keepdims=True)
            p = jnp.exp2((s - top) * (SCALE * LOG2E)).astype(BF)
            o = mm(p, va)
            att[rows, hcols] = (o[:, :HD] / o[:, HD:]).astype(BF)

    copies = [fen_out]
    for b in range(qs.shape[0] // ROWS):
        for g in range(KV_HEADS):
            attend(b, g)
        rows = pl.ds(b * ROWS, ROWS)
        cp = pltpu.make_async_copy(att.at[rows], att_hbm.at[rows], out_sem.at[1 + b])
        cp.start()
        copies.append(cp)
    for cp in copies:
        cp.wait()


def shards(
    queries, key_rows, value_rows, level_codes, level_coefs, norm_gain, w_query, w_key, w_value,
    lookback,
):
    tok, feat = queries.shape
    levels = level_codes.shape[1]
    d_model = w_query.shape[0]
    kvd = w_key.shape[1]
    seg = tok // N_HEAD
    chunks = tok // CHUNK
    hbm = pl.BlockSpec(memory_space=pltpu.HBM)
    vmem = pl.BlockSpec(memory_space=pltpu.VMEM)
    dma = pltpu.SemaphoreType.DMA
    mid = pl.pallas_call(
        body,
        out_shape=(
            pltpu.VMEM((tok, feat), BF),
            pltpu.VMEM((seg, d_model), BF),
            pltpu.VMEM((seg + WIN, 2 * kvd), BF),
            pltpu.VMEM((seg // ROWS, ROWS, WIN + ROWS), F32),
        ),
        in_specs=[hbm] * 10,
        out_specs=(vmem,) * 4,
        scratch_shapes=[
            pltpu.VMEM((tok, feat), BF),
            pltpu.VMEM((tok, feat), BF),
            pltpu.VMEM((tok, feat), BF),
            pltpu.VMEM((feat, tok), BF),
            pltpu.VMEM((feat, tok), BF),
            pltpu.VMEM((levels, tok), jnp.int32),
            pltpu.SMEM((HERE, NCOEF), F32),
            pltpu.VMEM((HERE, HD), F32),
            pltpu.VMEM((feat, HD), F32),
            pltpu.VMEM((seg // ROWS, ROWS), jnp.int32),
            pltpu.VMEM((HERE, levels, tok), F32),
            pltpu.VMEM((HALF, HALF), jnp.int32),
            pltpu.VMEM((feat, tok), F32),
            pltpu.VMEM((chunks, feat, HD), F32),
            pltpu.VMEM((7, feat, HD), BF),
            pltpu.VMEM((feat, HD), F32),
            pltpu.VMEM((feat, HD), BF),
            pltpu.VMEM((feat, HD), BF),
            pltpu.VMEM((SIDE, feat // 2, HD), BF),
            pltpu.VMEM((SIDE, feat // 2, HD), BF),
            pltpu.VMEM((feat, FAR * HD), BF),
            pltpu.VMEM((seg, d_model), BF),
            pltpu.VMEM((d_model, d_model + 2 * kvd), BF),
            pltpu.VMEM((CHUNK, feat), BF),
            pltpu.VMEM((CHUNK, d_model + 2 * kvd), F32),
            dma((5, 2)), dma((3,)), dma((4,)),
            dma((1,)), dma((1,)), dma((SIDE,)), dma((SIDE,)), dma((SIDE,)), dma((SIDE,)),
            dma((2,)), dma((2,)), dma((2, N_HEAD)), dma((2, N_HEAD)), dma((1,)), dma((1,)),
            dma((1,)), dma((1,)),
        ],
        compiler_params=pltpu.CompilerParams(
            collective_id=0, has_side_effects=True, vmem_limit_bytes=50 << 20
        ),
    )(
        queries, key_rows, value_rows, level_codes.T, level_coefs,
        norm_gain.reshape(HERE, HD), w_query, w_key, w_value, lookback.reshape(seg // ROWS, ROWS),
    )
    return pl.pallas_call(
        attention,
        out_shape=(
            jax.ShapeDtypeStruct((tok, feat), BF),
            jax.ShapeDtypeStruct((seg, d_model), BF),
        ),
        in_specs=[vmem] * 4,
        out_specs=(hbm, hbm),
        scratch_shapes=[pltpu.VMEM((seg, d_model), BF), dma((1 + seg // ROWS,))],
        compiler_params=pltpu.CompilerParams(vmem_limit_bytes=32 << 20),
    )(*mid)


def solution(mesh):
    in_specs = (
        P("ctx", "head"),
        P("ctx", "head"),
        P("ctx", "head"),
        P("ctx", None),
        P("head", None),
        P("head"),
        P(),
        P(),
        P(),
        P(("ctx", "head")),
    )
    out_specs = (P("ctx", "head"), P(("ctx", "head"), None))
    return jax.shard_map(shards, mesh=mesh, in_specs=in_specs, out_specs=out_specs, check_vma=False)
```

```python
import functools

import jax
import jax.numpy as jnp
from jax import lax
from jax.experimental import pallas as pl
from jax.experimental.pallas import tpu as pltpu
from jax.sharding import PartitionSpec as P

HD = 128
HEADS = 16
KV_HEADS = 4
GROUPS = HEADS // KV_HEADS
WIN = 256
NCOEF = 16
N_HEAD = 4
SIDE = 4
FAR = 5
HERE = HEADS // N_HEAD
CHUNK = 256
HALF = CHUNK // 2
ROWS = 128
NEAR_BITS = 8
MESH = pl.DeviceIdType.MESH
BF = jnp.bfloat16
F32 = jnp.float32
SCALE = HD ** (-0.5)
PLAN = ((7,), (5,), (3,), (1,), (6, 4, 2, 0))
LOG2E = 1.4426950408889634


def mm(a, b):
    return jnp.dot(a, b, preferred_element_type=F32)


def mm_nt(a, b):
    return lax.dot_general(a, b, (((1,), (1,)), ((), ())), preferred_element_type=F32)


def body(
    q_hbm, k_hbm, v_hbm, codes_hbm, coef_hbm, gain_hbm, wq_hbm, wk_hbm, wv_hbm, look_hbm,
    fen, qs, kvb, bias,
    q_v, k_v, v_v, qt, vt, codes, coef, gain, gain_t, look, lam, lev, loc, cst, lst,
    tot, totb, crecv, xr, yr, far, xg, w_v, relay, part,
    in_sem, w_sem, small_sem,
    core_ss, core_rs, x_ss, x_rs, y_ss, y_rs, f_ss, f_rs, z_ss, z_rs, h_ss, h_rs, r_ss, r_rs,
):
    tok = q_hbm.shape[0]
    chunks = tok // CHUNK
    seg = tok // N_HEAD
    d_model = wq_hbm.shape[0]
    kvd = wk_hbm.shape[1]
    feat = HERE * HD
    n_ctx = lax.axis_size("ctx")

    c = lax.axis_index("ctx")
    z = lax.axis_index("head")
    core = lax.rem(c, 2)
    cx = lax.rem(c // 2, SIDE)
    cy = c // (2 * SIDE)
    shard = c * N_HEAD + z

    def at_x(v):
        return (cy * 2 * SIDE + v * 2 + core, z)

    def at_y(v):
        return (v * 2 * SIDE + cx * 2 + core, z)

    def at_z(v):
        return (c, v)

    other_core = (c + 1 - 2 * core, z)
    nshard = n_ctx * N_HEAD
    nxt = lax.rem(shard + 1, nshard)
    prv = lax.rem(shard + nshard - 1, nshard)
    next_dev = (nxt // N_HEAD, lax.rem(nxt, N_HEAD))
    prev_dev = (prv // N_HEAD, lax.rem(prv, N_HEAD))

    barrier = pltpu.get_barrier_semaphore()
    friends = [other_core, next_dev, prev_dev]
    for s in range(1, SIDE):
        friends.append(at_x(lax.rem(cx + s, SIDE)))
        friends.append(at_y(lax.rem(cy + s, SIDE)))
        friends.append(at_z(lax.rem(z + s, N_HEAD)))
    for dev in friends:
        pl.semaphore_signal(barrier, inc=1, device_id=dev, device_id_type=MESH)

    quarter = tok // 4
    first = []
    for n in range(4):
        rows = pl.ds(n * quarter, quarter)
        pair = []
        for a, (src, dst) in enumerate(((v_hbm, v_v), (k_hbm, k_v))):
            cp = pltpu.make_async_copy(src.at[rows], dst.at[rows], in_sem.at[n, a])
            cp.start()
            pair.append(cp)
        first.append(pair)
    small = []
    for a, (src, dst) in enumerate(
        ((codes_hbm, codes), (coef_hbm, coef), (gain_hbm, gain), (look_hbm, look))
    ):
        cp = pltpu.make_async_copy(src, dst, small_sem.at[a])
        cp.start()
        small.append(cp)
    q_in = pltpu.make_async_copy(q_hbm, q_v, in_sem.at[4, 0])
    q_in.start()
    def pair_states(b):
        for n in range(4):
            if b == 0:
                for cp in first[n]:
                    cp.wait()

            def state_step(i, carry):
                rows = pl.ds(pl.multiple_of(i * CHUNK, CHUNK), CHUNK)
                for h in (2 * b, 2 * b + 1):
                    hs = slice(h * HD, (h + 1) * HD)
                    vtc = v_v[rows, hs].T
                    vt[hs, rows] = vtc
                    cst[i, hs, :] = mm(vtc, k_v[rows, hs])
                return carry

            lax.fori_loop(n * chunks // 4, (n + 1) * chunks // 4, state_step, 0)
        hs = slice(2 * b * HD, (2 * b + 2) * HD)
        pairs = [cst[2 * j, hs, :] + cst[2 * j + 1, hs, :] for j in range(4)]
        lo4 = pairs[0] + pairs[1]
        total = lo4 + (pairs[2] + pairs[3])
        tot[hs, :] = total
        totb[hs, :] = total.astype(BF)
        for j in range(4):
            lst[j, hs, :] = cst[2 * j, hs, :].astype(BF)
        lst[4, hs, :] = pairs[0].astype(BF)
        lst[5, hs, :] = pairs[2].astype(BF)
        lst[6, hs, :] = lo4.astype(BF)

    def core_copy(b):
        hs = pl.ds(2 * b * HD, 2 * HD)
        return pltpu.make_async_remote_copy(
            src_ref=totb.at[hs], dst_ref=crecv.at[hs], send_sem=core_ss.at[b], recv_sem=core_rs.at[b],
            device_id=other_core, device_id_type=MESH,
        )

    def mine(b):
        return pl.ds(pl.multiple_of((2 * b + core) * HD, HD), HD)

    def spread(buf, b, own, place, sends, recvs):
        out = []
        for s in (2, 1, 3):
            cp = pltpu.make_async_remote_copy(
                src_ref=buf.at[b, own], dst_ref=buf.at[b, own],
                send_sem=sends.at[b, s], recv_sem=recvs.at[b, s],
                device_id=place(lax.rem(own + s, SIDE)), device_id_type=MESH,
            )
            cp.start()
            out.append(cp)
        return out

    def chip_sum(b):
        core_cps[b].wait_recv()
        rows = mine(b)
        xr[b, cx] = (tot[rows, :] + crecv[rows, :].astype(F32)).astype(BF)
        return spread(xr, b, cx, at_x, x_ss, x_rs)

    pair_states(0)
    pl.semaphore_wait(barrier, len(friends))
    core_cps = [core_copy(0), core_copy(1)]
    core_cps[0].start()
    pair_states(1)
    core_cps[1].start()
    x_cps = [chip_sum(0)]
    w_in = [
        pltpu.make_async_copy(wk_hbm, w_v.at[:, pl.ds(d_model, kvd)], w_sem.at[0]),
        pltpu.make_async_copy(wv_hbm, w_v.at[:, pl.ds(d_model + kvd, kvd)], w_sem.at[1]),
        pltpu.make_async_copy(wq_hbm, w_v.at[:, pl.ds(0, d_model)], w_sem.at[2]),
    ]
    for cp in w_in:
        cp.start()

    for cp in small:
        cp.wait()
    si = lax.broadcasted_iota(jnp.int32, (HALF, HALF), 0)
    ti = lax.broadcasted_iota(jnp.int32, (HALF, HALF), 1)
    diff = jnp.bitwise_xor(si, ti)
    level = jnp.zeros((HALF, HALF), jnp.int32)
    for b in range(NEAR_BITS - 1):
        level = level + jnp.where(diff >= (1 << b), 1, 0)
    lev[...] = jnp.where(si <= ti, level, 99)
    for h in range(HERE):
        gain_t[h * HD : (h + 1) * HD, :] = jnp.broadcast_to(gain[h : h + 1, :], (HD, HD)).T

    x_cps.append(chip_sum(1))
    far[:, 0:HD] = jnp.where(core == 1, crecv[...].astype(F32), 0.0).astype(BF)

    def lam_step(i, carry):
        cols = pl.ds(pl.multiple_of(i * CHUNK, CHUNK), CHUNK)
        cd = codes[:, cols]
        for h in range(HERE):
            acc = jnp.full(cd.shape, coef[h, 0], F32)
            for n in range(1, NCOEF):
                acc = jnp.where(cd == n, coef[h, n], acc)
            lam[h, :, cols] = acc
        return carry

    lax.fori_loop(0, chunks, lam_step, 0)
    q_in.wait()

    def q_step(i, carry):
        rows = pl.ds(pl.multiple_of(i * CHUNK, CHUNK), CHUNK)
        qt[:, rows] = q_v[rows, :].T
        return carry

    lax.fori_loop(0, chunks, q_step, 0)

    def local_chunk(i):
        t0 = i * CHUNK
        cols = slice(t0, t0 + CHUNK)

        def head(h, carry):
            hoff = pl.multiple_of(h * HD, HD)
            hrows = pl.ds(hoff, HD)
            qth = qt[hrows, cols]
            st = mm(k_v[cols, hrows], qth)
            lamh = lam.at[h]

            def quad(a):
                lo = t0 + a * HALF
                w = jnp.zeros((HALF, HALF), F32)
                lv = lev[...]
                for l in range(NEAR_BITS):
                    w = jnp.where(lv == l, lamh[l : l + 1, lo : lo + HALF], w)
                return (st[a * HALF : (a + 1) * HALF, a * HALF : (a + 1) * HALF] * w).astype(BF)

            cross = (
                st[:HALF, HALF:] * lamh[NEAR_BITS : NEAR_BITS + 1, t0 + HALF : t0 + CHUNK]
            ).astype(BF)
            top = jnp.concatenate([quad(0), cross], axis=1)
            low = jnp.concatenate([jnp.zeros((HALF, HALF), BF), quad(1)], axis=1)
            terms = jnp.concatenate([top, low], axis=0)
            acc = mm(vt[hrows, cols], terms)
            used = []
            if i & 1:
                used.append((i // 2, 9))
            if i & 2:
                used.append((4 + i // 4, 10))
            if i & 4:
                used.append((6, 11))
            for slot, l in used:
                ql = qth * jnp.broadcast_to(lamh[l : l + 1, cols], (HD, CHUNK)).astype(BF)
                acc = acc + mm(lst[slot, hrows, :], ql)
            loc[hrows, cols] = acc
            return carry

        lax.fori_loop(0, HERE, head, 0, unroll=2)

    def m(cond):
        return jnp.where(cond, 1.0, 0.0).astype(F32)

    def level_pair(buf, b, pos, n, cps):
        for cp in cps:
            cp.wait_recv()
        parts = [buf[b, j].astype(F32) for j in range(SIDE)]
        low = parts[0] + parts[1]
        one = parts[0] * m(pos == 1) + parts[2] * m(pos == 3)
        two = low * m(pos >= 2)
        if n == 0:
            yr[b, cy] = (low + (parts[2] + parts[3])).astype(BF)
            y_cps.append(spread(yr, b, cy, at_y, y_ss, y_rs))
        rows = mine(b)
        far[rows, (2 * n + 1) * HD : (2 * n + 2) * HD] = one.astype(BF)
        far[rows, (2 * n + 2) * HD : (2 * n + 3) * HD] = two.astype(BF)
        piece = far.at[rows, pl.ds((2 * n + 1) * HD, 2 * HD)]
        cp = pltpu.make_async_remote_copy(
            src_ref=piece, dst_ref=piece, send_sem=f_ss.at[n, b], recv_sem=f_rs.at[n, b],
            device_id=other_core, device_id_type=MESH,
        )
        cp.start()
        f_cps[b].append(cp)

    y_cps = []
    f_cps = [[], []]
    for i in PLAN[0]:
        local_chunk(i)
    level_pair(xr, 0, cx, 0, x_cps[0])
    for i in PLAN[1]:
        local_chunk(i)
    level_pair(xr, 1, cx, 0, x_cps[1])
    for i in PLAN[2]:
        local_chunk(i)
    level_pair(yr, 0, cy, 1, y_cps[0])
    for i in PLAN[3]:
        local_chunk(i)

    def to_z(k):
        return lax.rem(z + k, N_HEAD)

    def z_copy(hf, k, b):
        dest = to_z(k)
        width = feat if b is None else feat // 2
        first_col = 0 if b is None else b * (feat // 2)
        slot = hf if b is None else 1 + b
        return pltpu.make_async_remote_copy(
            src_ref=fen.at[
                pl.ds(pl.multiple_of(dest * seg + hf * CHUNK, CHUNK), CHUNK), pl.ds(first_col, width)
            ],
            dst_ref=xg.at[
                pl.ds(hf * CHUNK, CHUNK),
                pl.ds(pl.multiple_of(z * feat + first_col, feat // 2), width),
            ],
            send_sem=z_ss.at[slot, k],
            recv_sem=z_rs.at[slot, k],
            device_id=at_z(dest),
            device_id_type=MESH,
        )

    def far_step(n, hf, b):
        k = jnp.where(n == 0, 2, jnp.where(n == 1, 1, jnp.where(n == 2, 3, 0)))
        cols = pl.ds(pl.multiple_of(to_z(k) * seg + hf * CHUNK, CHUNK), CHUNK)
        for h in range(HERE) if b is None else (2 * b, 2 * b + 1):
            hs = slice(h * HD, (h + 1) * HD)
            qth = qt[hs, cols]
            parts = []
            for l in range(FAR):
                row = lam[h, 12 + l : 13 + l, cols]
                parts.append(qth * jnp.broadcast_to(row, (HD, CHUNK)).astype(BF))
            acc = loc[hs, cols] + mm(far[hs, :], jnp.concatenate(parts, axis=0))
            ms = jnp.sum(acc * acc, axis=0, keepdims=True)
            r = SCALE * lax.rsqrt(ms * (SCALE * SCALE / HD) + 1e-06)
            g = gain_t[hs, :]
            g = jnp.concatenate([g, g], axis=1)
            fen[cols, hs] = (acc * r * g).astype(BF).T

        if hf == 1:

            @pl.when(k > 0)
            def _():
                z_copy(1, k, b).start()

        @pl.when((k == 0) & (b != 0))
        def _():
            xg[
                pl.ds(hf * CHUNK, CHUNK),
                pl.ds(pl.multiple_of(z * feat, feat), feat),
            ] = fen[cols, :]

    def far_loop(hf, b):
        def step(n, carry):
            far_step(n, hf, b)
            return carry

        lax.fori_loop(0, N_HEAD, step, 0)

    for cp in f_cps[0]:
        cp.wait()
    far_loop(1, 0)
    level_pair(yr, 1, cy, 1, y_cps[1])
    for cp in f_cps[1]:
        cp.wait()
    far_loop(1, 1)
    for i in PLAN[4]:
        local_chunk(i)
    far_loop(0, None)

    hop = pltpu.make_async_remote_copy(
        src_ref=fen.at[pl.ds(pl.multiple_of(to_z(2) * seg, CHUNK), CHUNK)],
        dst_ref=relay,
        send_sem=r_ss.at[0], recv_sem=r_rs.at[0],
        device_id=at_z(to_z(3)), device_id_type=MESH,
    )
    hop.start()
    z_copy(0, 1, None).start()
    z_copy(0, 3, None).start()
    onward = pltpu.make_async_remote_copy(
        src_ref=relay,
        dst_ref=xg.at[pl.ds(0, CHUNK), pl.ds(pl.multiple_of(to_z(1) * feat, feat), feat)],
        send_sem=z_ss.at[0, 2], recv_sem=z_rs.at[0, 2],
        device_id=at_z(to_z(3)), device_id_type=MESH,
    )
    halo = pltpu.make_async_remote_copy(
        src_ref=kvb.at[pl.ds(seg, WIN)], dst_ref=kvb.at[pl.ds(0, WIN)],
        send_sem=h_ss.at[0], recv_sem=h_rs.at[0], device_id=next_dev, device_id_type=MESH,
    )
    ri = lax.broadcasted_iota(jnp.int32, (ROWS, WIN + ROWS), 0)
    ji = lax.broadcasted_iota(jnp.int32, (ROWS, WIN + ROWS), 1)
    gap = WIN + ri - ji
    for b in range(seg // ROWS):
        reach = jnp.broadcast_to(look[b : b + 1, :].astype(F32), (ROWS, ROWS)).T
        reach = jnp.concatenate([reach] * 3, axis=1).astype(jnp.int32)
        key_pos = shard * seg + b * ROWS - WIN + ji
        ok = (gap >= 0) & (gap <= reach) & (key_pos >= 0)
        bias[b] = jnp.where(ok, 0.0, -1e30)

    for cp in w_in:
        cp.wait()

    for b in range(2):
        for k in (1, 3, 2):
            z_copy(1, k, b).wait_recv()
    late = slice(CHUNK, 2 * CHUNK)
    for n in range(2):
        wcols = slice(d_model + n * kvd, d_model + (n + 1) * kvd)
        kvb[WIN + CHUNK :, n * kvd : (n + 1) * kvd] = mm(xg[late, :], w_v[:, wcols]).astype(BF)
    halo.start()

    def q_proj(n, carry):
        off = pl.ds(pl.multiple_of(n * kvd, kvd), kvd)
        qs[late, off] = mm(xg[late, :], w_v[:, off]).astype(BF)
        return carry

    lax.fori_loop(0, d_model // kvd, q_proj, 0)
    hop.wait_recv()
    onward.start()

    def two(j, k, off):
        total = None
        for s in (j, k):
            fs = pl.ds(pl.multiple_of(lax.rem(z + N_HEAD - s, N_HEAD) * feat, feat), feat)
            term = mm(xg[0:CHUNK, fs], w_v[fs, off])
            total = term if total is None else total + term
        return total

    z_copy(0, 1, None).wait_recv()

    def part_step(n, carry):
        off = pl.ds(pl.multiple_of(n * kvd, kvd), kvd)
        part[:, off] = two(0, 1, off)
        return carry

    lax.fori_loop(0, d_model // kvd + 2, part_step, 0)
    z_copy(0, 3, None).wait_recv()
    onward.wait_recv()
    for n in range(2):
        wcols = pl.ds(d_model + n * kvd, kvd)
        kvb[WIN : WIN + CHUNK, n * kvd : (n + 1) * kvd] = (part[:, wcols] + two(3, 2, wcols)).astype(BF)

    def q_rest(n, carry):
        off = pl.ds(pl.multiple_of(n * kvd, kvd), kvd)
        qs[0:CHUNK, off] = (part[:, off] + two(3, 2, off)).astype(BF)
        return carry

    lax.fori_loop(0, d_model // kvd, q_rest, 0)

    halo.wait_recv()
    for cp in core_cps + x_cps[0] + x_cps[1] + y_cps[0] + y_cps[1]:
        cp.wait_send()
    for b in range(2):
        for k in (1, 3, 2):
            z_copy(1, k, b).wait_send()
    z_copy(0, 1, None).wait_send()
    z_copy(0, 3, None).wait_send()
    hop.wait_send()
    onward.wait_send()
    halo.wait_send()


def attention(fen, qs, kvb, bias, fen_hbm, att_hbm, att, out_sem):
    kvd = kvb.shape[1] // 2
    fen_out = pltpu.make_async_copy(fen, fen_hbm, out_sem.at[0])
    fen_out.start()
    ones = jnp.ones((WIN + ROWS, HD), BF)

    def attend(b, g):
        rows = slice(b * ROWS, (b + 1) * ROWS)
        keys = slice(b * ROWS, b * ROWS + WIN + ROWS)
        kg = kvb[keys, g * HD : (g + 1) * HD]
        vg = kvb[keys, kvd + g * HD : kvd + (g + 1) * HD]
        va = jnp.concatenate([vg, ones], axis=1)
        mask = bias[b]
        for i in range(GROUPS):
            hcols = slice((g * GROUPS + i) * HD, (g * GROUPS + i + 1) * HD)
            s = mm_nt(qs[rows, hcols], kg) + mask
            top = jnp.max(s, axis=1, keepdims=True)
            p = jnp.exp2((s - top) * (SCALE * LOG2E)).astype(BF)
            o = mm(p, va)
            att[rows, hcols] = (o[:, :HD] / o[:, HD:]).astype(BF)

    copies = [fen_out]
    for b in range(qs.shape[0] // ROWS):
        for g in range(KV_HEADS):
            attend(b, g)
        rows = pl.ds(b * ROWS, ROWS)
        cp = pltpu.make_async_copy(att.at[rows], att_hbm.at[rows], out_sem.at[1 + b])
        cp.start()
        copies.append(cp)
    for cp in copies:
        cp.wait()


def shards(
    queries, key_rows, value_rows, level_codes, level_coefs, norm_gain, w_query, w_key, w_value,
    lookback,
):
    tok, feat = queries.shape
    levels = level_codes.shape[1]
    d_model = w_query.shape[0]
    kvd = w_key.shape[1]
    seg = tok // N_HEAD
    chunks = tok // CHUNK
    hbm = pl.BlockSpec(memory_space=pltpu.HBM)
    vmem = pl.BlockSpec(memory_space=pltpu.VMEM)
    dma = pltpu.SemaphoreType.DMA
    mid = pl.pallas_call(
        body,
        out_shape=(
            pltpu.VMEM((tok, feat), BF),
            pltpu.VMEM((seg, d_model), BF),
            pltpu.VMEM((seg + WIN, 2 * kvd), BF),
            pltpu.VMEM((seg // ROWS, ROWS, WIN + ROWS), F32),
        ),
        in_specs=[hbm] * 10,
        out_specs=(vmem,) * 4,
        scratch_shapes=[
            pltpu.VMEM((tok, feat), BF),
            pltpu.VMEM((tok, feat), BF),
            pltpu.VMEM((tok, feat), BF),
            pltpu.VMEM((feat, tok), BF),
            pltpu.VMEM((feat, tok), BF),
            pltpu.VMEM((levels, tok), jnp.int32),
            pltpu.SMEM((HERE, NCOEF), F32),
            pltpu.VMEM((HERE, HD), F32),
            pltpu.VMEM((feat, HD), F32),
            pltpu.VMEM((seg // ROWS, ROWS), jnp.int32),
            pltpu.VMEM((HERE, levels, tok), F32),
            pltpu.VMEM((HALF, HALF), jnp.int32),
            pltpu.VMEM((feat, tok), F32),
            pltpu.VMEM((chunks, feat, HD), F32),
            pltpu.VMEM((7, feat, HD), BF),
            pltpu.VMEM((feat, HD), F32),
            pltpu.VMEM((feat, HD), BF),
            pltpu.VMEM((feat, HD), BF),
            pltpu.VMEM((2, SIDE, HD, HD), BF),
            pltpu.VMEM((2, SIDE, HD, HD), BF),
            pltpu.VMEM((feat, FAR * HD), BF),
            pltpu.VMEM((seg, d_model), BF),
            pltpu.VMEM((d_model, d_model + 2 * kvd), BF),
            pltpu.VMEM((CHUNK, feat), BF),
            pltpu.VMEM((CHUNK, d_model + 2 * kvd), F32),
            dma((5, 2)), dma((3,)), dma((4,)),
            dma((2,)), dma((2,)), dma((2, SIDE)), dma((2, SIDE)), dma((2, SIDE)), dma((2, SIDE)),
            dma((2, 2)), dma((2, 2)), dma((3, N_HEAD)), dma((3, N_HEAD)), dma((1,)), dma((1,)),
            dma((1,)), dma((1,)),
        ],
        compiler_params=pltpu.CompilerParams(
            collective_id=0, has_side_effects=True, vmem_limit_bytes=50 << 20
        ),
    )(
        queries, key_rows, value_rows, level_codes.T, level_coefs,
        norm_gain.reshape(HERE, HD), w_query, w_key, w_value, lookback.reshape(seg // ROWS, ROWS),
    )
    return pl.pallas_call(
        attention,
        out_shape=(
            jax.ShapeDtypeStruct((tok, feat), BF),
            jax.ShapeDtypeStruct((seg, d_model), BF),
        ),
        in_specs=[vmem] * 4,
        out_specs=(hbm, hbm),
        scratch_shapes=[pltpu.VMEM((seg, d_model), BF), dma((1 + seg // ROWS,))],
        compiler_params=pltpu.CompilerParams(vmem_limit_bytes=32 << 20),
    )(*mid)


def solution(mesh):
    in_specs = (
        P("ctx", "head"),
        P("ctx", "head"),
        P("ctx", "head"),
        P("ctx", None),
        P("head", None),
        P("head"),
        P(),
        P(),
        P(),
        P(("ctx", "head")),
    )
    out_specs = (P("ctx", "head"), P(("ctx", "head"), None))
    return jax.shard_map(shards, mesh=mesh, in_specs=in_specs, out_specs=out_specs, check_vma=False)
```

```python
import functools

import jax
import jax.numpy as jnp
from jax import lax
from jax.experimental import pallas as pl
from jax.experimental.pallas import tpu as pltpu
from jax.sharding import PartitionSpec as P

HD = 128
HEADS = 16
KV_HEADS = 4
GROUPS = HEADS // KV_HEADS
WIN = 256
NCOEF = 16
N_HEAD = 4
SIDE = 4
FAR = 5
HERE = HEADS // N_HEAD
CHUNK = 256
HALF = CHUNK // 2
ROWS = 128
NEAR_BITS = 8
MESH = pl.DeviceIdType.MESH
BF = jnp.bfloat16
F32 = jnp.float32
SCALE = HD ** (-0.5)
PLAN = ((7,), (5,), (3,), (1,))
LOG2E = 1.4426950408889634


def mm(a, b):
    return jnp.dot(a, b, preferred_element_type=F32)


def mm_nt(a, b):
    return lax.dot_general(a, b, (((1,), (1,)), ((), ())), preferred_element_type=F32)


def body(
    q_hbm, k_hbm, v_hbm, codes_hbm, coef_hbm, gain_hbm, wq_hbm, wk_hbm, wv_hbm, look_hbm,
    fen, qs, kvb, bias,
    q_v, k_v, v_v, qt, vt, codes, coef, gain, gain_t, look, lam, lev, loc, cst, lst,
    tot, totb, crecv, xr, yr, far, xg, w_v, relay, part,
    in_sem, w_sem, small_sem,
    core_ss, core_rs, x_ss, x_rs, y_ss, y_rs, f_ss, f_rs, z_ss, z_rs, h_ss, h_rs, r_ss, r_rs,
):
    tok = q_hbm.shape[0]
    chunks = tok // CHUNK
    seg = tok // N_HEAD
    d_model = wq_hbm.shape[0]
    kvd = wk_hbm.shape[1]
    feat = HERE * HD
    n_ctx = lax.axis_size("ctx")

    c = lax.axis_index("ctx")
    z = lax.axis_index("head")
    core = lax.rem(c, 2)
    cx = lax.rem(c // 2, SIDE)
    cy = c // (2 * SIDE)
    shard = c * N_HEAD + z

    def at_x(v):
        return (cy * 2 * SIDE + v * 2 + core, z)

    def at_y(v):
        return (v * 2 * SIDE + cx * 2 + core, z)

    def at_z(v):
        return (c, v)

    other_core = (c + 1 - 2 * core, z)
    nshard = n_ctx * N_HEAD
    nxt = lax.rem(shard + 1, nshard)
    prv = lax.rem(shard + nshard - 1, nshard)
    next_dev = (nxt // N_HEAD, lax.rem(nxt, N_HEAD))
    prev_dev = (prv // N_HEAD, lax.rem(prv, N_HEAD))

    barrier = pltpu.get_barrier_semaphore()
    friends = [other_core, next_dev, prev_dev]
    for s in range(1, SIDE):
        friends.append(at_x(lax.rem(cx + s, SIDE)))
        friends.append(at_y(lax.rem(cy + s, SIDE)))
        friends.append(at_z(lax.rem(z + s, N_HEAD)))
    for dev in friends:
        pl.semaphore_signal(barrier, inc=1, device_id=dev, device_id_type=MESH)

    quarter = tok // 4
    first = []
    for n in range(4):
        rows = pl.ds(n * quarter, quarter)
        pair = []
        for a, (src, dst) in enumerate(((v_hbm, v_v), (k_hbm, k_v))):
            cp = pltpu.make_async_copy(src.at[rows], dst.at[rows], in_sem.at[n, a])
            cp.start()
            pair.append(cp)
        first.append(pair)
    small = []
    for a, (src, dst) in enumerate(
        ((codes_hbm, codes), (coef_hbm, coef), (gain_hbm, gain), (look_hbm, look))
    ):
        cp = pltpu.make_async_copy(src, dst, small_sem.at[a])
        cp.start()
        small.append(cp)
    q_in = pltpu.make_async_copy(q_hbm, q_v, in_sem.at[4, 0])
    q_in.start()
    def pair_states(b):
        for n in range(4):
            if b == 0:
                for cp in first[n]:
                    cp.wait()

            def state_step(i, carry):
                rows = pl.ds(pl.multiple_of(i * CHUNK, CHUNK), CHUNK)
                for h in (2 * b, 2 * b + 1):
                    hs = slice(h * HD, (h + 1) * HD)
                    vtc = v_v[rows, hs].T
                    vt[hs, rows] = vtc
                    cst[i, hs, :] = mm(vtc, k_v[rows, hs])
                return carry

            lax.fori_loop(n * chunks // 4, (n + 1) * chunks // 4, state_step, 0)
        hs = slice(2 * b * HD, (2 * b + 2) * HD)
        pairs = [cst[2 * j, hs, :] + cst[2 * j + 1, hs, :] for j in range(4)]
        lo4 = pairs[0] + pairs[1]
        total = lo4 + (pairs[2] + pairs[3])
        tot[hs, :] = total
        totb[hs, :] = total.astype(BF)
        for j in range(4):
            lst[j, hs, :] = cst[2 * j, hs, :].astype(BF)
        lst[4, hs, :] = pairs[0].astype(BF)
        lst[5, hs, :] = pairs[2].astype(BF)
        lst[6, hs, :] = lo4.astype(BF)

    def core_copy(b):
        hs = pl.ds(2 * b * HD, 2 * HD)
        return pltpu.make_async_remote_copy(
            src_ref=totb.at[hs], dst_ref=crecv.at[hs], send_sem=core_ss.at[b], recv_sem=core_rs.at[b],
            device_id=other_core, device_id_type=MESH,
        )

    def mine(b):
        return pl.ds(pl.multiple_of((2 * b + core) * HD, HD), HD)

    def spread(buf, b, own, place, sends, recvs):
        out = []
        for s in (2, 1, 3):
            cp = pltpu.make_async_remote_copy(
                src_ref=buf.at[b, own], dst_ref=buf.at[b, own],
                send_sem=sends.at[b, s], recv_sem=recvs.at[b, s],
                device_id=place(lax.rem(own + s, SIDE)), device_id_type=MESH,
            )
            cp.start()
            out.append(cp)
        return out

    def chip_sum(b):
        core_cps[b].wait_recv()
        rows = mine(b)
        xr[b, cx] = (tot[rows, :] + crecv[rows, :].astype(F32)).astype(BF)
        return spread(xr, b, cx, at_x, x_ss, x_rs)

    pair_states(0)
    pl.semaphore_wait(barrier, len(friends))
    core_cps = [core_copy(0), core_copy(1)]
    core_cps[0].start()
    pair_states(1)
    core_cps[1].start()
    x_cps = [chip_sum(0)]
    w_in = [
        pltpu.make_async_copy(wk_hbm, w_v.at[:, pl.ds(d_model, kvd)], w_sem.at[0]),
        pltpu.make_async_copy(wv_hbm, w_v.at[:, pl.ds(d_model + kvd, kvd)], w_sem.at[1]),
        pltpu.make_async_copy(wq_hbm, w_v.at[:, pl.ds(0, d_model)], w_sem.at[2]),
    ]
    for cp in w_in:
        cp.start()

    for cp in small:
        cp.wait()
    si = lax.broadcasted_iota(jnp.int32, (HALF, HALF), 0)
    ti = lax.broadcasted_iota(jnp.int32, (HALF, HALF), 1)
    diff = jnp.bitwise_xor(si, ti)
    level = jnp.zeros((HALF, HALF), jnp.int32)
    for b in range(NEAR_BITS - 1):
        level = level + jnp.where(diff >= (1 << b), 1, 0)
    lev[...] = jnp.where(si <= ti, level, 99)
    for h in range(HERE):
        gain_t[h * HD : (h + 1) * HD, :] = jnp.broadcast_to(gain[h : h + 1, :], (HD, HD)).T

    x_cps.append(chip_sum(1))
    far[:, 0:HD] = jnp.where(core == 1, crecv[...].astype(F32), 0.0).astype(BF)

    def lam_step(i, carry):
        cols = pl.ds(pl.multiple_of(i * CHUNK, CHUNK), CHUNK)
        cd = codes[:, cols]
        for h in range(HERE):
            acc = jnp.full(cd.shape, coef[h, 0], F32)
            for n in range(1, NCOEF):
                acc = jnp.where(cd == n, coef[h, n], acc)
            lam[h, :, cols] = acc
        return carry

    lax.fori_loop(0, chunks, lam_step, 0)
    q_in.wait()

    def q_step(i, carry):
        rows = pl.ds(pl.multiple_of(i * CHUNK, CHUNK), CHUNK)
        qt[:, rows] = q_v[rows, :].T
        return carry

    lax.fori_loop(0, chunks, q_step, 0)

    def m(cond):
        return jnp.where(cond, 1.0, 0.0).astype(F32)

    def local_chunk(i):
        fixed = isinstance(i, int)
        t0 = i * CHUNK if fixed else pl.multiple_of(i * CHUNK, CHUNK)
        cols = pl.ds(t0, CHUNK)

        def head(h, carry):
            hoff = pl.multiple_of(h * HD, HD)
            hrows = pl.ds(hoff, HD)
            qth = qt[hrows, cols]
            st = mm(k_v[cols, hrows], qth)
            lamh = lam.at[h]

            def quad(a):
                lo = t0 + a * HALF
                lo = lo if fixed else pl.multiple_of(lo, HALF)
                w = jnp.zeros((HALF, HALF), F32)
                lv = lev[...]
                for l in range(NEAR_BITS):
                    w = jnp.where(lv == l, lamh[l : l + 1, pl.ds(lo, HALF)], w)
                return (st[a * HALF : (a + 1) * HALF, a * HALF : (a + 1) * HALF] * w).astype(BF)

            cross = (
                st[:HALF, HALF:] * lamh[NEAR_BITS : NEAR_BITS + 1, pl.ds(t0 + HALF if fixed else pl.multiple_of(t0 + HALF, HALF), HALF)]
            ).astype(BF)
            top = jnp.concatenate([quad(0), cross], axis=1)
            low = jnp.concatenate([jnp.zeros((HALF, HALF), BF), quad(1)], axis=1)
            terms = jnp.concatenate([top, low], axis=0)
            acc = mm(vt[hrows, cols], terms)
            used = []
            if fixed:
                if i & 1:
                    used.append((i // 2, 9, None))
                if i & 2:
                    used.append((4 + i // 4, 10, None))
                if i & 4:
                    used.append((6, 11, None))
            else:
                used.append((4 + i // 4, 10, m(lax.rem(i // 2, 2) == 1)))
                used.append((6, 11, m(i >= 4)))
            for slot, l, keep in used:
                row = lamh[l : l + 1, cols]
                row = row if keep is None else row * keep
                acc = acc + mm(lst[slot, hrows, :], qth * jnp.broadcast_to(row, (HD, CHUNK)).astype(BF))
            loc[hrows, cols] = acc
            return carry

        lax.fori_loop(0, HERE, head, 0, unroll=2)

    def level_pair(buf, b, pos, n, cps):
        for cp in cps:
            cp.wait_recv()
        parts = [buf[b, j].astype(F32) for j in range(SIDE)]
        low = parts[0] + parts[1]
        one = parts[0] * m(pos == 1) + parts[2] * m(pos == 3)
        two = low * m(pos >= 2)
        if n == 0:
            yr[b, cy] = (low + (parts[2] + parts[3])).astype(BF)
            y_cps.append(spread(yr, b, cy, at_y, y_ss, y_rs))
        rows = mine(b)
        far[rows, (2 * n + 1) * HD : (2 * n + 2) * HD] = one.astype(BF)
        far[rows, (2 * n + 2) * HD : (2 * n + 3) * HD] = two.astype(BF)
        piece = far.at[rows, pl.ds((2 * n + 1) * HD, 2 * HD)]
        cp = pltpu.make_async_remote_copy(
            src_ref=piece, dst_ref=piece, send_sem=f_ss.at[n, b], recv_sem=f_rs.at[n, b],
            device_id=other_core, device_id_type=MESH,
        )
        cp.start()
        f_cps[b].append(cp)

    y_cps = []
    f_cps = [[], []]
    for i in PLAN[0]:
        local_chunk(i)
    level_pair(xr, 0, cx, 0, x_cps[0])
    for i in PLAN[1]:
        local_chunk(i)
    level_pair(xr, 1, cx, 0, x_cps[1])
    for i in PLAN[2]:
        local_chunk(i)
    level_pair(yr, 0, cy, 1, y_cps[0])
    for i in PLAN[3]:
        local_chunk(i)

    def to_z(k):
        return lax.rem(z + k, N_HEAD)

    def z_copy(hf, k, b):
        dest = to_z(k)
        width = feat if b is None else feat // 2
        first_col = 0 if b is None else b * (feat // 2)
        slot = hf if b is None else 1 + b
        return pltpu.make_async_remote_copy(
            src_ref=fen.at[
                pl.ds(pl.multiple_of(dest * seg + hf * CHUNK, CHUNK), CHUNK), pl.ds(first_col, width)
            ],
            dst_ref=xg.at[
                pl.ds(hf * CHUNK, CHUNK),
                pl.ds(pl.multiple_of(z * feat + first_col, feat // 2), width),
            ],
            send_sem=z_ss.at[slot, k],
            recv_sem=z_rs.at[slot, k],
            device_id=at_z(dest),
            device_id_type=MESH,
        )

    def far_step(n, hf, b):
        k = jnp.where(n == 0, 2, jnp.where(n == 1, 1, jnp.where(n == 2, 3, 0)))
        cols = pl.ds(pl.multiple_of(to_z(k) * seg + hf * CHUNK, CHUNK), CHUNK)
        for h in range(HERE) if b is None else (2 * b, 2 * b + 1):
            hs = slice(h * HD, (h + 1) * HD)
            qth = qt[hs, cols]
            parts = []
            for l in range(FAR):
                row = lam[h, 12 + l : 13 + l, cols]
                parts.append(qth * jnp.broadcast_to(row, (HD, CHUNK)).astype(BF))
            acc = loc[hs, cols] + mm(far[hs, :], jnp.concatenate(parts, axis=0))
            ms = jnp.sum(acc * acc, axis=0, keepdims=True)
            r = SCALE * lax.rsqrt(ms * (SCALE * SCALE / HD) + 1e-06)
            g = gain_t[hs, :]
            g = jnp.concatenate([g, g], axis=1)
            fen[cols, hs] = (acc * r * g).astype(BF).T

        if hf == 1:

            @pl.when(k > 0)
            def _():
                z_copy(1, k, b).start()

        @pl.when((k == 0) & (b != 0))
        def _():
            xg[
                pl.ds(hf * CHUNK, CHUNK),
                pl.ds(pl.multiple_of(z * feat, feat), feat),
            ] = fen[cols, :]

    def far_loop(hf, b):
        def step(n, carry):
            far_step(n, hf, b)
            return carry

        lax.fori_loop(0, N_HEAD, step, 0)

    for cp in f_cps[0]:
        cp.wait()
    far_loop(1, 0)
    level_pair(yr, 1, cy, 1, y_cps[1])
    for cp in f_cps[1]:
        cp.wait()
    far_loop(1, 1)

    hop = pltpu.make_async_remote_copy(
        src_ref=fen.at[pl.ds(pl.multiple_of(to_z(2) * seg, CHUNK), CHUNK)],
        dst_ref=relay,
        send_sem=r_ss.at[0], recv_sem=r_rs.at[0],
        device_id=at_z(to_z(3)), device_id_type=MESH,
    )

    def first_half(n, carry):
        k = jnp.where(n == 0, 2, jnp.where(n == 1, 1, jnp.where(n == 2, 3, 0)))
        local_chunk(2 * to_z(k))
        far_step(n, 0, None)

        @pl.when(n == 0)
        def _():
            hop.start()

        @pl.when((n == 1) | (n == 2))
        def _():
            z_copy(0, k, None).start()

        return carry

    lax.fori_loop(0, N_HEAD, first_half, 0)
    onward = pltpu.make_async_remote_copy(
        src_ref=relay,
        dst_ref=xg.at[pl.ds(0, CHUNK), pl.ds(pl.multiple_of(to_z(1) * feat, feat), feat)],
        send_sem=z_ss.at[0, 2], recv_sem=z_rs.at[0, 2],
        device_id=at_z(to_z(3)), device_id_type=MESH,
    )
    halo = pltpu.make_async_remote_copy(
        src_ref=kvb.at[pl.ds(seg, WIN)], dst_ref=kvb.at[pl.ds(0, WIN)],
        send_sem=h_ss.at[0], recv_sem=h_rs.at[0], device_id=next_dev, device_id_type=MESH,
    )
    ri = lax.broadcasted_iota(jnp.int32, (ROWS, WIN + ROWS), 0)
    ji = lax.broadcasted_iota(jnp.int32, (ROWS, WIN + ROWS), 1)
    gap = WIN + ri - ji
    for b in range(seg // ROWS):
        reach = jnp.broadcast_to(look[b : b + 1, :].astype(F32), (ROWS, ROWS)).T
        reach = jnp.concatenate([reach] * 3, axis=1).astype(jnp.int32)
        key_pos = shard * seg + b * ROWS - WIN + ji
        ok = (gap >= 0) & (gap <= reach) & (key_pos >= 0)
        bias[b] = jnp.where(ok, 0.0, -1e30)

    for cp in w_in:
        cp.wait()

    for b in range(2):
        for k in (1, 3, 2):
            z_copy(1, k, b).wait_recv()
    late = slice(CHUNK, 2 * CHUNK)
    for n in range(2):
        wcols = slice(d_model + n * kvd, d_model + (n + 1) * kvd)
        kvb[WIN + CHUNK :, n * kvd : (n + 1) * kvd] = mm(xg[late, :], w_v[:, wcols]).astype(BF)
    halo.start()
    hop.wait_recv()
    onward.start()

    def q_proj(n, carry):
        off = pl.ds(pl.multiple_of(n * kvd, kvd), kvd)
        qs[late, off] = mm(xg[late, :], w_v[:, off]).astype(BF)
        return carry

    lax.fori_loop(0, d_model // kvd, q_proj, 0)

    def two(j, k, off):
        total = None
        for s in (j, k):
            fs = pl.ds(pl.multiple_of(lax.rem(z + N_HEAD - s, N_HEAD) * feat, feat), feat)
            term = mm(xg[0:CHUNK, fs], w_v[fs, off])
            total = term if total is None else total + term
        return total

    z_copy(0, 1, None).wait_recv()

    def part_step(n, carry):
        off = pl.ds(pl.multiple_of(n * kvd, kvd), kvd)
        part[:, off] = two(0, 1, off)
        return carry

    lax.fori_loop(0, d_model // kvd + 2, part_step, 0)
    z_copy(0, 3, None).wait_recv()
    onward.wait_recv()
    for n in range(2):
        wcols = pl.ds(d_model + n * kvd, kvd)
        kvb[WIN : WIN + CHUNK, n * kvd : (n + 1) * kvd] = (part[:, wcols] + two(3, 2, wcols)).astype(BF)

    def q_rest(n, carry):
        off = pl.ds(pl.multiple_of(n * kvd, kvd), kvd)
        qs[0:CHUNK, off] = (part[:, off] + two(3, 2, off)).astype(BF)
        return carry

    lax.fori_loop(0, d_model // kvd, q_rest, 0)

    halo.wait_recv()
    for cp in core_cps + x_cps[0] + x_cps[1] + y_cps[0] + y_cps[1]:
        cp.wait_send()
    for b in range(2):
        for k in (1, 3, 2):
            z_copy(1, k, b).wait_send()
    z_copy(0, 1, None).wait_send()
    z_copy(0, 3, None).wait_send()
    hop.wait_send()
    onward.wait_send()
    halo.wait_send()


def attention(fen, qs, kvb, bias, fen_hbm, att_hbm, att, out_sem):
    kvd = kvb.shape[1] // 2
    fen_out = pltpu.make_async_copy(fen, fen_hbm, out_sem.at[0])
    fen_out.start()
    ones = jnp.ones((WIN + ROWS, HD), BF)

    def attend(b, g):
        rows = slice(b * ROWS, (b + 1) * ROWS)
        keys = slice(b * ROWS, b * ROWS + WIN + ROWS)
        kg = kvb[keys, g * HD : (g + 1) * HD]
        vg = kvb[keys, kvd + g * HD : kvd + (g + 1) * HD]
        va = jnp.concatenate([vg, ones], axis=1)
        mask = bias[b]
        for i in range(GROUPS):
            hcols = slice((g * GROUPS + i) * HD, (g * GROUPS + i + 1) * HD)
            s = mm_nt(qs[rows, hcols], kg) + mask
            top = jnp.max(s, axis=1, keepdims=True)
            p = jnp.exp2((s - top) * (SCALE * LOG2E)).astype(BF)
            o = mm(p, va)
            att[rows, hcols] = (o[:, :HD] / o[:, HD:]).astype(BF)

    copies = [fen_out]
    for b in range(qs.shape[0] // ROWS):
        for g in range(KV_HEADS):
            attend(b, g)
        rows = pl.ds(b * ROWS, ROWS)
        cp = pltpu.make_async_copy(att.at[rows], att_hbm.at[rows], out_sem.at[1 + b])
        cp.start()
        copies.append(cp)
    for cp in copies:
        cp.wait()


def shards(
    queries, key_rows, value_rows, level_codes, level_coefs, norm_gain, w_query, w_key, w_value,
    lookback,
):
    tok, feat = queries.shape
    levels = level_codes.shape[1]
    d_model = w_query.shape[0]
    kvd = w_key.shape[1]
    seg = tok // N_HEAD
    chunks = tok // CHUNK
    hbm = pl.BlockSpec(memory_space=pltpu.HBM)
    vmem = pl.BlockSpec(memory_space=pltpu.VMEM)
    dma = pltpu.SemaphoreType.DMA
    mid = pl.pallas_call(
        body,
        out_shape=(
            pltpu.VMEM((tok, feat), BF),
            pltpu.VMEM((seg, d_model), BF),
            pltpu.VMEM((seg + WIN, 2 * kvd), BF),
            pltpu.VMEM((seg // ROWS, ROWS, WIN + ROWS), F32),
        ),
        in_specs=[hbm] * 10,
        out_specs=(vmem,) * 4,
        scratch_shapes=[
            pltpu.VMEM((tok, feat), BF),
            pltpu.VMEM((tok, feat), BF),
            pltpu.VMEM((tok, feat), BF),
            pltpu.VMEM((feat, tok), BF),
            pltpu.VMEM((feat, tok), BF),
            pltpu.VMEM((levels, tok), jnp.int32),
            pltpu.SMEM((HERE, NCOEF), F32),
            pltpu.VMEM((HERE, HD), F32),
            pltpu.VMEM((feat, HD), F32),
            pltpu.VMEM((seg // ROWS, ROWS), jnp.int32),
            pltpu.VMEM((HERE, levels, tok), F32),
            pltpu.VMEM((HALF, HALF), jnp.int32),
            pltpu.VMEM((feat, tok), F32),
            pltpu.VMEM((chunks, feat, HD), F32),
            pltpu.VMEM((7, feat, HD), BF),
            pltpu.VMEM((feat, HD), F32),
            pltpu.VMEM((feat, HD), BF),
            pltpu.VMEM((feat, HD), BF),
            pltpu.VMEM((2, SIDE, HD, HD), BF),
            pltpu.VMEM((2, SIDE, HD, HD), BF),
            pltpu.VMEM((feat, FAR * HD), BF),
            pltpu.VMEM((seg, d_model), BF),
            pltpu.VMEM((d_model, d_model + 2 * kvd), BF),
            pltpu.VMEM((CHUNK, feat), BF),
            pltpu.VMEM((CHUNK, d_model + 2 * kvd), F32),
            dma((5, 2)), dma((3,)), dma((4,)),
            dma((2,)), dma((2,)), dma((2, SIDE)), dma((2, SIDE)), dma((2, SIDE)), dma((2, SIDE)),
            dma((2, 2)), dma((2, 2)), dma((3, N_HEAD)), dma((3, N_HEAD)), dma((1,)), dma((1,)),
            dma((1,)), dma((1,)),
        ],
        compiler_params=pltpu.CompilerParams(
            collective_id=0, has_side_effects=True, vmem_limit_bytes=50 << 20
        ),
    )(
        queries, key_rows, value_rows, level_codes.T, level_coefs,
        norm_gain.reshape(HERE, HD), w_query, w_key, w_value, lookback.reshape(seg // ROWS, ROWS),
    )
    return pl.pallas_call(
        attention,
        out_shape=(
            jax.ShapeDtypeStruct((tok, feat), BF),
            jax.ShapeDtypeStruct((seg, d_model), BF),
        ),
        in_specs=[vmem] * 4,
        out_specs=(hbm, hbm),
        scratch_shapes=[pltpu.VMEM((seg, d_model), BF), dma((1 + seg // ROWS,))],
        compiler_params=pltpu.CompilerParams(vmem_limit_bytes=32 << 20),
    )(*mid)


def solution(mesh):
    in_specs = (
        P("ctx", "head"),
        P("ctx", "head"),
        P("ctx", "head"),
        P("ctx", None),
        P("head", None),
        P("head"),
        P(),
        P(),
        P(),
        P(("ctx", "head")),
    )
    out_specs = (P("ctx", "head"), P(("ctx", "head"), None))
    return jax.shard_map(shards, mesh=mesh, in_specs=in_specs, out_specs=out_specs, check_vma=False)
```

```python
import functools

import jax
import jax.numpy as jnp
from jax import lax
from jax.experimental import pallas as pl
from jax.experimental.pallas import tpu as pltpu
from jax.sharding import PartitionSpec as P

HD = 128
HEADS = 16
KV_HEADS = 4
GROUPS = HEADS // KV_HEADS
WIN = 256
NCOEF = 16
N_HEAD = 4
SIDE = 4
FAR = 5
HERE = HEADS // N_HEAD
CHUNK = 256
HALF = CHUNK // 2
ROWS = 128
NEAR_BITS = 8
MESH = pl.DeviceIdType.MESH
BF = jnp.bfloat16
F32 = jnp.float32
SCALE = HD ** (-0.5)
PLAN = ((7,), (5,), (3,), (1,))
LOG2E = 1.4426950408889634


def mm(a, b):
    return jnp.dot(a, b, preferred_element_type=F32)


def mm_nt(a, b):
    return lax.dot_general(a, b, (((1,), (1,)), ((), ())), preferred_element_type=F32)


def body(
    q_hbm, k_hbm, v_hbm, codes_hbm, coef_hbm, gain_hbm, wq_hbm, wk_hbm, wv_hbm, look_hbm,
    fen, qs, kvb, bias,
    q_v, k_v, v_v, qt, vt, codes, coef, gain, gain_t, look, lam, lev, loc, cst, lst,
    tot, totb, crecv, xr, yr, far, xg, w_v, relay, part,
    in_sem, w_sem, small_sem,
    core_ss, core_rs, x_ss, x_rs, y_ss, y_rs, f_ss, f_rs, z_ss, z_rs, h_ss, h_rs, r_ss, r_rs,
):
    tok = q_hbm.shape[0]
    chunks = tok // CHUNK
    seg = tok // N_HEAD
    d_model = wq_hbm.shape[0]
    kvd = wk_hbm.shape[1]
    feat = HERE * HD
    n_ctx = lax.axis_size("ctx")

    c = lax.axis_index("ctx")
    z = lax.axis_index("head")
    core = lax.rem(c, 2)
    cx = lax.rem(c // 2, SIDE)
    cy = c // (2 * SIDE)
    shard = c * N_HEAD + z

    def at_x(v):
        return (cy * 2 * SIDE + v * 2 + core, z)

    def at_y(v):
        return (v * 2 * SIDE + cx * 2 + core, z)

    def at_z(v):
        return (c, v)

    other_core = (c + 1 - 2 * core, z)
    nshard = n_ctx * N_HEAD
    nxt = lax.rem(shard + 1, nshard)
    prv = lax.rem(shard + nshard - 1, nshard)
    next_dev = (nxt // N_HEAD, lax.rem(nxt, N_HEAD))
    prev_dev = (prv // N_HEAD, lax.rem(prv, N_HEAD))

    barrier = pltpu.get_barrier_semaphore()
    friends = [other_core, next_dev, prev_dev]
    for s in range(1, SIDE):
        friends.append(at_x(lax.rem(cx + s, SIDE)))
        friends.append(at_y(lax.rem(cy + s, SIDE)))
        friends.append(at_z(lax.rem(z + s, N_HEAD)))
    for dev in friends:
        pl.semaphore_signal(barrier, inc=1, device_id=dev, device_id_type=MESH)

    quarter = tok // 4
    first = []
    for n in range(4):
        rows = pl.ds(n * quarter, quarter)
        pair = []
        for a, (src, dst) in enumerate(((v_hbm, v_v), (k_hbm, k_v))):
            cp = pltpu.make_async_copy(src.at[rows], dst.at[rows], in_sem.at[n, a])
            cp.start()
            pair.append(cp)
        first.append(pair)
    small = []
    for a, (src, dst) in enumerate(
        ((codes_hbm, codes), (coef_hbm, coef), (gain_hbm, gain), (look_hbm, look))
    ):
        cp = pltpu.make_async_copy(src, dst, small_sem.at[a])
        cp.start()
        small.append(cp)
    q_in = pltpu.make_async_copy(q_hbm, q_v, in_sem.at[4, 0])
    q_in.start()
    def pair_states(b):
        for n in range(4):
            if b == 0:
                for cp in first[n]:
                    cp.wait()

            def state_step(i, carry):
                rows = pl.ds(pl.multiple_of(i * CHUNK, CHUNK), CHUNK)
                for h in (2 * b, 2 * b + 1):
                    hs = slice(h * HD, (h + 1) * HD)
                    vtc = v_v[rows, hs].T
                    vt[hs, rows] = vtc
                    cst[i, hs, :] = mm(vtc, k_v[rows, hs])
                return carry

            lax.fori_loop(n * chunks // 4, (n + 1) * chunks // 4, state_step, 0, unroll=2)
        hs = slice(2 * b * HD, (2 * b + 2) * HD)
        pairs = [cst[2 * j, hs, :] + cst[2 * j + 1, hs, :] for j in range(4)]
        lo4 = pairs[0] + pairs[1]
        total = lo4 + (pairs[2] + pairs[3])
        tot[hs, :] = total
        totb[hs, :] = total.astype(BF)
        for j in range(4):
            lst[j, hs, :] = cst[2 * j, hs, :].astype(BF)
        lst[4, hs, :] = pairs[0].astype(BF)
        lst[5, hs, :] = pairs[2].astype(BF)
        lst[6, hs, :] = lo4.astype(BF)

    def core_copy(b):
        hs = pl.ds(2 * b * HD, 2 * HD)
        return pltpu.make_async_remote_copy(
            src_ref=totb.at[hs], dst_ref=crecv.at[hs], send_sem=core_ss.at[b], recv_sem=core_rs.at[b],
            device_id=other_core, device_id_type=MESH,
        )

    def mine(b):
        return pl.ds(pl.multiple_of((2 * b + core) * HD, HD), HD)

    def spread(buf, b, own, place, sends, recvs):
        out = []
        for s in (2, 1, 3):
            cp = pltpu.make_async_remote_copy(
                src_ref=buf.at[b, own], dst_ref=buf.at[b, own],
                send_sem=sends.at[b, s], recv_sem=recvs.at[b, s],
                device_id=place(lax.rem(own + s, SIDE)), device_id_type=MESH,
            )
            cp.start()
            out.append(cp)
        return out

    def chip_sum(b):
        core_cps[b].wait_recv()
        rows = mine(b)
        xr[b, cx] = (tot[rows, :] + crecv[rows, :].astype(F32)).astype(BF)
        return spread(xr, b, cx, at_x, x_ss, x_rs)

    pair_states(0)
    pl.semaphore_wait(barrier, len(friends))
    core_cps = [core_copy(0), core_copy(1)]
    core_cps[0].start()
    pair_states(1)
    core_cps[1].start()
    x_cps = [chip_sum(0)]
    w_in = [
        pltpu.make_async_copy(wk_hbm, w_v.at[:, pl.ds(d_model, kvd)], w_sem.at[0]),
        pltpu.make_async_copy(wv_hbm, w_v.at[:, pl.ds(d_model + kvd, kvd)], w_sem.at[1]),
        pltpu.make_async_copy(wq_hbm, w_v.at[:, pl.ds(0, d_model)], w_sem.at[2]),
    ]
    for cp in w_in:
        cp.start()

    for cp in small:
        cp.wait()
    si = lax.broadcasted_iota(jnp.int32, (HALF, HALF), 0)
    ti = lax.broadcasted_iota(jnp.int32, (HALF, HALF), 1)
    diff = jnp.bitwise_xor(si, ti)
    level = jnp.zeros((HALF, HALF), jnp.int32)
    for b in range(NEAR_BITS - 1):
        level = level + jnp.where(diff >= (1 << b), 1, 0)
    lev[...] = jnp.where(si <= ti, level, 99)
    for h in range(HERE):
        gain_t[h * HD : (h + 1) * HD, :] = jnp.broadcast_to(gain[h : h + 1, :], (HD, HD)).T

    x_cps.append(chip_sum(1))
    far[:, 0:HD] = jnp.where(core == 1, crecv[...].astype(F32), 0.0).astype(BF)

    def lam_step(i, carry):
        cols = pl.ds(pl.multiple_of(i * CHUNK, CHUNK), CHUNK)
        cd = codes[:, cols]
        for h in range(HERE):
            acc = jnp.full(cd.shape, coef[h, 0], F32)
            for n in range(1, NCOEF):
                acc = jnp.where(cd == n, coef[h, n], acc)
            lam[h, :, cols] = acc
        return carry

    lax.fori_loop(0, chunks, lam_step, 0)
    q_in.wait()

    def q_step(i, carry):
        rows = pl.ds(pl.multiple_of(i * CHUNK, CHUNK), CHUNK)
        qt[:, rows] = q_v[rows, :].T
        return carry

    lax.fori_loop(0, chunks, q_step, 0)

    def m(cond):
        return jnp.where(cond, 1.0, 0.0).astype(F32)

    def local_chunk(i):
        fixed = isinstance(i, int)
        t0 = i * CHUNK if fixed else pl.multiple_of(i * CHUNK, CHUNK)
        cols = pl.ds(t0, CHUNK)

        def head(h, carry):
            hoff = pl.multiple_of(h * HD, HD)
            hrows = pl.ds(hoff, HD)
            qth = qt[hrows, cols]
            st = mm(k_v[cols, hrows], qth)
            lamh = lam.at[h]

            def quad(a):
                lo = t0 + a * HALF
                lo = lo if fixed else pl.multiple_of(lo, HALF)
                w = jnp.zeros((HALF, HALF), F32)
                lv = lev[...]
                for l in range(NEAR_BITS):
                    w = jnp.where(lv == l, lamh[l : l + 1, pl.ds(lo, HALF)], w)
                return (st[a * HALF : (a + 1) * HALF, a * HALF : (a + 1) * HALF] * w).astype(BF)

            cross = (
                st[:HALF, HALF:] * lamh[NEAR_BITS : NEAR_BITS + 1, pl.ds(t0 + HALF if fixed else pl.multiple_of(t0 + HALF, HALF), HALF)]
            ).astype(BF)
            top = jnp.concatenate([quad(0), cross], axis=1)
            low = jnp.concatenate([jnp.zeros((HALF, HALF), BF), quad(1)], axis=1)
            terms = jnp.concatenate([top, low], axis=0)
            acc = mm(vt[hrows, cols], terms)
            used = []
            if fixed:
                if i & 1:
                    used.append((i // 2, 9, None))
                if i & 2:
                    used.append((4 + i // 4, 10, None))
                if i & 4:
                    used.append((6, 11, None))
            else:
                used.append((4 + i // 4, 10, m(lax.rem(i // 2, 2) == 1)))
                used.append((6, 11, m(i >= 4)))
            for slot, l, keep in used:
                row = lamh[l : l + 1, cols]
                row = row if keep is None else row * keep
                acc = acc + mm(lst[slot, hrows, :], qth * jnp.broadcast_to(row, (HD, CHUNK)).astype(BF))
            loc[hrows, cols] = acc
            return carry

        lax.fori_loop(0, HERE, head, 0, unroll=2)

    def level_pair(buf, b, pos, n, cps):
        for cp in cps:
            cp.wait_recv()
        parts = [buf[b, j].astype(F32) for j in range(SIDE)]
        low = parts[0] + parts[1]
        one = parts[0] * m(pos == 1) + parts[2] * m(pos == 3)
        two = low * m(pos >= 2)
        if n == 0:
            yr[b, cy] = (low + (parts[2] + parts[3])).astype(BF)
            y_cps.append(spread(yr, b, cy, at_y, y_ss, y_rs))
        rows = mine(b)
        far[rows, (2 * n + 1) * HD : (2 * n + 2) * HD] = one.astype(BF)
        far[rows, (2 * n + 2) * HD : (2 * n + 3) * HD] = two.astype(BF)
        piece = far.at[rows, pl.ds((2 * n + 1) * HD, 2 * HD)]
        cp = pltpu.make_async_remote_copy(
            src_ref=piece, dst_ref=piece, send_sem=f_ss.at[n, b], recv_sem=f_rs.at[n, b],
            device_id=other_core, device_id_type=MESH,
        )
        cp.start()
        f_cps[b].append(cp)

    y_cps = []
    f_cps = [[], []]
    for i in PLAN[0]:
        local_chunk(i)
    level_pair(xr, 0, cx, 0, x_cps[0])
    for i in PLAN[1]:
        local_chunk(i)
    level_pair(xr, 1, cx, 0, x_cps[1])
    for i in PLAN[2]:
        local_chunk(i)
    level_pair(yr, 0, cy, 1, y_cps[0])
    for i in PLAN[3]:
        local_chunk(i)

    def to_z(k):
        return lax.rem(z + k, N_HEAD)

    def z_copy(hf, k, b):
        dest = to_z(k)
        width = feat if b is None else feat // 2
        first_col = 0 if b is None else b * (feat // 2)
        slot = hf if b is None else 1 + b
        return pltpu.make_async_remote_copy(
            src_ref=fen.at[
                pl.ds(pl.multiple_of(dest * seg + hf * CHUNK, CHUNK), CHUNK), pl.ds(first_col, width)
            ],
            dst_ref=xg.at[
                pl.ds(hf * CHUNK, CHUNK),
                pl.ds(pl.multiple_of(z * feat + first_col, feat // 2), width),
            ],
            send_sem=z_ss.at[slot, k],
            recv_sem=z_rs.at[slot, k],
            device_id=at_z(dest),
            device_id_type=MESH,
        )

    def far_step(n, hf, b):
        k = jnp.where(n == 0, 2, jnp.where(n == 1, 1, jnp.where(n == 2, 3, 0)))
        cols = pl.ds(pl.multiple_of(to_z(k) * seg + hf * CHUNK, CHUNK), CHUNK)
        for h in range(HERE) if b is None else (2 * b, 2 * b + 1):
            hs = slice(h * HD, (h + 1) * HD)
            qth = qt[hs, cols]
            parts = []
            for l in range(FAR):
                row = lam[h, 12 + l : 13 + l, cols]
                parts.append(qth * jnp.broadcast_to(row, (HD, CHUNK)).astype(BF))
            acc = loc[hs, cols] + mm(far[hs, :], jnp.concatenate(parts, axis=0))
            ms = jnp.sum(acc * acc, axis=0, keepdims=True)
            r = SCALE * lax.rsqrt(ms * (SCALE * SCALE / HD) + 1e-06)
            g = gain_t[hs, :]
            g = jnp.concatenate([g, g], axis=1)
            fen[cols, hs] = (acc * r * g).astype(BF).T

        if hf == 1:

            @pl.when(k > 0)
            def _():
                z_copy(1, k, b).start()

        @pl.when((k == 0) & (b != 0))
        def _():
            xg[
                pl.ds(hf * CHUNK, CHUNK),
                pl.ds(pl.multiple_of(z * feat, feat), feat),
            ] = fen[cols, :]

    def far_loop(hf, b):
        def step(n, carry):
            far_step(n, hf, b)
            return carry

        lax.fori_loop(0, N_HEAD, step, 0)

    for cp in f_cps[0]:
        cp.wait()
    far_loop(1, 0)
    level_pair(yr, 1, cy, 1, y_cps[1])
    for cp in f_cps[1]:
        cp.wait()
    far_loop(1, 1)

    hop = pltpu.make_async_remote_copy(
        src_ref=fen.at[pl.ds(pl.multiple_of(to_z(2) * seg, CHUNK), CHUNK)],
        dst_ref=relay,
        send_sem=r_ss.at[0], recv_sem=r_rs.at[0],
        device_id=at_z(to_z(3)), device_id_type=MESH,
    )

    def first_half(n, carry):
        k = jnp.where(n == 0, 2, jnp.where(n == 1, 1, jnp.where(n == 2, 3, 0)))
        local_chunk(2 * to_z(k))
        far_step(n, 0, None)

        @pl.when(n == 0)
        def _():
            hop.start()

        @pl.when((n == 1) | (n == 2))
        def _():
            z_copy(0, k, None).start()

        return carry

    lax.fori_loop(0, N_HEAD, first_half, 0)
    onward = pltpu.make_async_remote_copy(
        src_ref=relay,
        dst_ref=xg.at[pl.ds(0, CHUNK), pl.ds(pl.multiple_of(to_z(1) * feat, feat), feat)],
        send_sem=z_ss.at[0, 2], recv_sem=z_rs.at[0, 2],
        device_id=at_z(to_z(3)), device_id_type=MESH,
    )
    halo = pltpu.make_async_remote_copy(
        src_ref=kvb.at[pl.ds(seg, WIN)], dst_ref=kvb.at[pl.ds(0, WIN)],
        send_sem=h_ss.at[0], recv_sem=h_rs.at[0], device_id=next_dev, device_id_type=MESH,
    )
    ri = lax.broadcasted_iota(jnp.int32, (ROWS, WIN + ROWS), 0)
    ji = lax.broadcasted_iota(jnp.int32, (ROWS, WIN + ROWS), 1)
    gap = WIN + ri - ji
    for b in range(seg // ROWS):
        reach = jnp.broadcast_to(look[b : b + 1, :].astype(F32), (ROWS, ROWS)).T
        reach = jnp.concatenate([reach] * 3, axis=1).astype(jnp.int32)
        key_pos = shard * seg + b * ROWS - WIN + ji
        ok = (gap >= 0) & (gap <= reach) & (key_pos >= 0)
        bias[b] = jnp.where(ok, 0.0, -1e30)

    for cp in w_in:
        cp.wait()

    for b in range(2):
        for k in (1, 3, 2):
            z_copy(1, k, b).wait_recv()
    late = slice(CHUNK, 2 * CHUNK)
    for n in range(2):
        wcols = slice(d_model + n * kvd, d_model + (n + 1) * kvd)
        kvb[WIN + CHUNK :, n * kvd : (n + 1) * kvd] = mm(xg[late, :], w_v[:, wcols]).astype(BF)
    halo.start()
    hop.wait_recv()
    onward.start()

    def q_proj(n, carry):
        off = pl.ds(pl.multiple_of(n * kvd, kvd), kvd)
        qs[late, off] = mm(xg[late, :], w_v[:, off]).astype(BF)
        return carry

    lax.fori_loop(0, d_model // kvd, q_proj, 0)

    def two(j, k, off):
        total = None
        for s in (j, k):
            fs = pl.ds(pl.multiple_of(lax.rem(z + N_HEAD - s, N_HEAD) * feat, feat), feat)
            term = mm(xg[0:CHUNK, fs], w_v[fs, off])
            total = term if total is None else total + term
        return total

    z_copy(0, 1, None).wait_recv()

    def part_step(n, carry):
        off = pl.ds(pl.multiple_of(n * kvd, kvd), kvd)
        part[:, off] = two(0, 1, off)
        return carry

    lax.fori_loop(0, d_model // kvd + 2, part_step, 0)
    z_copy(0, 3, None).wait_recv()
    onward.wait_recv()
    for n in range(2):
        wcols = pl.ds(d_model + n * kvd, kvd)
        kvb[WIN : WIN + CHUNK, n * kvd : (n + 1) * kvd] = (part[:, wcols] + two(3, 2, wcols)).astype(BF)

    def q_rest(n, carry):
        off = pl.ds(pl.multiple_of(n * kvd, kvd), kvd)
        qs[0:CHUNK, off] = (part[:, off] + two(3, 2, off)).astype(BF)
        return carry

    lax.fori_loop(0, d_model // kvd, q_rest, 0)

    halo.wait_recv()
    for cp in core_cps + x_cps[0] + x_cps[1] + y_cps[0] + y_cps[1]:
        cp.wait_send()
    for b in range(2):
        for k in (1, 3, 2):
            z_copy(1, k, b).wait_send()
    z_copy(0, 1, None).wait_send()
    z_copy(0, 3, None).wait_send()
    hop.wait_send()
    onward.wait_send()
    halo.wait_send()


def attention(fen, qs, kvb, bias, fen_hbm, att_hbm, att, out_sem):
    kvd = kvb.shape[1] // 2
    fen_out = pltpu.make_async_copy(fen, fen_hbm, out_sem.at[0])
    fen_out.start()
    ones = jnp.ones((WIN + ROWS, HD), BF)

    def attend(b, g):
        rows = slice(b * ROWS, (b + 1) * ROWS)
        keys = slice(b * ROWS, b * ROWS + WIN + ROWS)
        kg = kvb[keys, g * HD : (g + 1) * HD]
        vg = kvb[keys, kvd + g * HD : kvd + (g + 1) * HD]
        va = jnp.concatenate([vg, ones], axis=1)
        mask = bias[b]
        for i in range(GROUPS):
            hcols = slice((g * GROUPS + i) * HD, (g * GROUPS + i + 1) * HD)
            s = mm_nt(qs[rows, hcols], kg) + mask
            top = jnp.max(s, axis=1, keepdims=True)
            p = jnp.exp2((s - top) * (SCALE * LOG2E)).astype(BF)
            o = mm(p, va)
            att[rows, hcols] = (o[:, :HD] / o[:, HD:]).astype(BF)

    copies = [fen_out]
    for b in range(qs.shape[0] // ROWS):
        rows = pl.ds(b * ROWS, ROWS)
        for g in range(KV_HEADS):
            attend(b, g)
            piece = (rows, pl.ds(g * GROUPS * HD, GROUPS * HD))
            cp = pltpu.make_async_copy(att.at[piece], att_hbm.at[piece], out_sem.at[1 + b * KV_HEADS + g])
            cp.start()
            copies.append(cp)
    for cp in copies:
        cp.wait()


def shards(
    queries, key_rows, value_rows, level_codes, level_coefs, norm_gain, w_query, w_key, w_value,
    lookback,
):
    tok, feat = queries.shape
    levels = level_codes.shape[1]
    d_model = w_query.shape[0]
    kvd = w_key.shape[1]
    seg = tok // N_HEAD
    chunks = tok // CHUNK
    hbm = pl.BlockSpec(memory_space=pltpu.HBM)
    vmem = pl.BlockSpec(memory_space=pltpu.VMEM)
    dma = pltpu.SemaphoreType.DMA
    mid = pl.pallas_call(
        body,
        out_shape=(
            pltpu.VMEM((tok, feat), BF),
            pltpu.VMEM((seg, d_model), BF),
            pltpu.VMEM((seg + WIN, 2 * kvd), BF),
            pltpu.VMEM((seg // ROWS, ROWS, WIN + ROWS), F32),
        ),
        in_specs=[hbm] * 10,
        out_specs=(vmem,) * 4,
        scratch_shapes=[
            pltpu.VMEM((tok, feat), BF),
            pltpu.VMEM((tok, feat), BF),
            pltpu.VMEM((tok, feat), BF),
            pltpu.VMEM((feat, tok), BF),
            pltpu.VMEM((feat, tok), BF),
            pltpu.VMEM((levels, tok), jnp.int32),
            pltpu.SMEM((HERE, NCOEF), F32),
            pltpu.VMEM((HERE, HD), F32),
            pltpu.VMEM((feat, HD), F32),
            pltpu.VMEM((seg // ROWS, ROWS), jnp.int32),
            pltpu.VMEM((HERE, levels, tok), F32),
            pltpu.VMEM((HALF, HALF), jnp.int32),
            pltpu.VMEM((feat, tok), F32),
            pltpu.VMEM((chunks, feat, HD), F32),
            pltpu.VMEM((7, feat, HD), BF),
            pltpu.VMEM((feat, HD), F32),
            pltpu.VMEM((feat, HD), BF),
            pltpu.VMEM((feat, HD), BF),
            pltpu.VMEM((2, SIDE, HD, HD), BF),
            pltpu.VMEM((2, SIDE, HD, HD), BF),
            pltpu.VMEM((feat, FAR * HD), BF),
            pltpu.VMEM((seg, d_model), BF),
            pltpu.VMEM((d_model, d_model + 2 * kvd), BF),
            pltpu.VMEM((CHUNK, feat), BF),
            pltpu.VMEM((CHUNK, d_model + 2 * kvd), F32),
            dma((5, 2)), dma((3,)), dma((4,)),
            dma((2,)), dma((2,)), dma((2, SIDE)), dma((2, SIDE)), dma((2, SIDE)), dma((2, SIDE)),
            dma((2, 2)), dma((2, 2)), dma((3, N_HEAD)), dma((3, N_HEAD)), dma((1,)), dma((1,)),
            dma((1,)), dma((1,)),
        ],
        compiler_params=pltpu.CompilerParams(
            collective_id=0, has_side_effects=True, vmem_limit_bytes=50 << 20
        ),
    )(
        queries, key_rows, value_rows, level_codes.T, level_coefs,
        norm_gain.reshape(HERE, HD), w_query, w_key, w_value, lookback.reshape(seg // ROWS, ROWS),
    )
    return pl.pallas_call(
        attention,
        out_shape=(
            jax.ShapeDtypeStruct((tok, feat), BF),
            jax.ShapeDtypeStruct((seg, d_model), BF),
        ),
        in_specs=[vmem] * 4,
        out_specs=(hbm, hbm),
        scratch_shapes=[pltpu.VMEM((seg, d_model), BF), dma((1 + seg // ROWS * KV_HEADS,))],
        compiler_params=pltpu.CompilerParams(vmem_limit_bytes=32 << 20),
    )(*mid)


def solution(mesh):
    in_specs = (
        P("ctx", "head"),
        P("ctx", "head"),
        P("ctx", "head"),
        P("ctx", None),
        P("head", None),
        P("head"),
        P(),
        P(),
        P(),
        P(("ctx", "head")),
    )
    out_specs = (P("ctx", "head"), P(("ctx", "head"), None))
    return jax.shard_map(shards, mesh=mesh, in_specs=in_specs, out_specs=out_specs, check_vma=False)
```
